512 devices in a mesh: gx: 8 (over y, z_hi), gy: 8 (over z_lo), gz: 8 (over x, core).
Axes of the slice: x: 4, y: 4, z: 16 (z_hi: 2, z_lo: 8; z = z_hi * 8 + z_lo), core: 2. Of those that a mesh axis runs over, the one named last changes fastest.
Arguments:
- attn_values: bfloat16 [3072, 4096], P('gy', ('gx', 'gz')), may hold values from -4 to 4
- attn_exponents: int32 [3072, 32], P('gy', 'gx'), may hold values from -4 to 0
- hidden_values: bfloat16 [3072, 14336], P('gy', ('gx', 'gz')), may hold values from -4 to 4
- hidden_exponents: int32 [3072, 112], P('gy', 'gx'), may hold values from -4 to 0
- attn_out_grad: bfloat16 [3072, 4096], P('gy', 'gz'), may hold values from -6 to 6
- mlp_out_grad: bfloat16 [3072, 4096], P('gy', 'gz'), may hold values from -6 to 6
- attn_weight: bfloat16 [4096, 4096], P(('gx', 'gy'), 'gz'), may hold values from -0.09375 to 0.09375
- mlp_weight: bfloat16 [14336, 4096], P(('gx', 'gy'), 'gz'), may hold values from -0.046875 to 0.046875
Outputs:
- attn_input_grad: bfloat16 [3072, 4096], P('gy', ('gx', 'gz'))
- mlp_input_grad: bfloat16 [3072, 14336], P('gy', ('gx', 'gz'))
- attn_weight_grad: bfloat16 [4096, 4096], P(('gx', 'gy'), 'gz')
- mlp_weight_grad: bfloat16 [14336, 4096], P(('gx', 'gy'), 'gz')
The draws below stay inside these ranges and needn't reach their ends.
All inputs are finite; a program needn't handle non-finite values.
Results may differ from the reference program's by a relative error of at most 0.017.
Values may be sent and summed in bfloat16 or wider, within the bound.
A program may use at most 64 MiB of HBM per device.

```python
import jax
import jax.numpy as jnp
from jax import lax

D = 4096
K_O = 4096
K_D = 14336
BLOCK = 128
TOK_DEV = 384
TOKENS = 3072
N_GY = 8
N_GZ = 8


def with_ends(drawn, key, smallest, high):
    dims = drawn.shape
    index_at = [jax.random.randint(jax.random.fold_in(key, axis), (), 0, dims[axis]) for axis in range(len(dims))]
    drawn = drawn.at[tuple(index_at)].set(smallest)
    longest = dims.index(max(dims))
    index_at[longest] = (index_at[longest] + 1) % dims[longest]
    return drawn.at[tuple(index_at)].set(high)


def strengthened(result, rng, source, target, shards_of, factor):
    def block_of(position):
        return (jnp.arange(result.shape[position]) // (result.shape[position] // shards_of)).reshape((-1,) + (1,) * (result.ndim - 1 - position))

    one_side = jax.random.permutation(rng, shards_of)[block_of(target)]
    far = (block_of(target) + shards_of // 2) % shards_of
    return jnp.where((block_of(source) == one_side) | (block_of(source) == far), factor * result, result)


def block_scale(rng, dims, shards, low, top_value):
    level, own = 1.0, jax.random.fold_in(rng, 6)
    for dim, blocks in shards:
        heights = jnp.exp(jax.random.uniform(jax.random.fold_in(own, dim), (blocks,), jnp.float32, low / len(shards), top_value / len(shards)))
        level = level * jnp.repeat(heights, dims[dim] // blocks).reshape([-1 if axis == dim else 1 for axis in range(len(dims))])
    return level


def normal_values(stream_key, shape, spread, limit, pieces=(), kind=jnp.bfloat16):
    entries = jax.random.normal(stream_key, shape, jnp.float32) * spread
    if len(pieces) > 0:
        entries = block_scale(stream_key, shape, pieces, -0.22, 0.18) * entries
    return jnp.clip(entries, min=-limit, max=limit).astype(kind)


def bell_draw_with(key, extent, scale, limit, shards, heavy, kind=jnp.bfloat16):
    entries = scale * jax.random.normal(key, extent, jnp.float32)
    if shards:
        entries = entries * block_scale(key, extent, shards, -0.22, 0.18)
    return jnp.clip(strengthened(entries, jax.random.fold_in(key, 3), *heavy), -limit, limit).astype(kind)


def setup_inputs(seed: int = 0) -> dict:
    seeds = jax.random.split(jax.random.key(seed), 9)
    attn_values = normal_values(seeds[0], (TOKENS, K_O), 1.0, 4.0, ((0, 8), (1, 64)))
    attn_exponents = with_ends(jax.random.randint(seeds[1], (TOKENS, K_O // BLOCK), -4, 1), jax.random.fold_in(seeds[1], 1), -4, 0).astype(jnp.int32)
    hidden_values = normal_values(seeds[2], (TOKENS, K_D), 1.0, 4.0, ((0, 8), (1, 64)))
    hidden_exponents = with_ends(jax.random.randint(seeds[3], (TOKENS, K_D // BLOCK), -4, 1), jax.random.fold_in(seeds[3], 1), -4, 0).astype(jnp.int32)
    attn_out_grad = bell_draw_with(seeds[4], (TOKENS, D), 1.0, 6.0, ((0, 8), (1, 8)), (1, 0, 8, 2.0))
    mlp_out_grad = bell_draw_with(seeds[5], (TOKENS, D), 1.0, 6.0, ((0, 8), (1, 8)), (1, 0, 8, 2.0))
    attn_weight = normal_values(seeds[6], (K_O, D), K_O ** -0.5, 0.09375, ((0, 64), (1, 8)))
    mlp_weight = normal_values(seeds[7], (K_D, D), K_D ** -0.5, 0.046875, ((0, 64), (1, 8)))
    return dict(attn_values=attn_values, attn_exponents=attn_exponents, hidden_values=hidden_values, hidden_exponents=hidden_exponents, attn_out_grad=attn_out_grad, mlp_out_grad=mlp_out_grad, attn_weight=attn_weight, mlp_weight=mlp_weight)


def dequantize(values, exponents):
    row_count, col_count = values.shape
    scales = jnp.exp2(exponents.astype(jnp.float32))
    widened = values.astype(jnp.float32).reshape(row_count, col_count // BLOCK, BLOCK) * scales[:, :, None]
    return widened.reshape(row_count, col_count).astype(jnp.bfloat16)

def rounded(partial_value):
    return lax.optimization_barrier(partial_value.astype(jnp.bfloat16)).astype(jnp.float32)

def input_grad(out_grad, weight):
    width = D // N_GZ
    total = jnp.zeros((out_grad.shape[0], weight.shape[0]), jnp.float32)
    for block_id in range(N_GZ):
        piece = out_grad[:, block_id * width:(block_id + 1) * width].astype(jnp.float32)
        columns = weight[:, block_id * width:(block_id + 1) * width].astype(jnp.float32)
        total = total + rounded(jnp.dot(piece, columns.T, precision=lax.Precision.HIGHEST))
    return total.astype(jnp.bfloat16)

def weight_grad(inputs, out_grad):
    total = jnp.zeros((inputs.shape[1], out_grad.shape[1]), jnp.float32)
    for block_id in range(N_GY):
        rows_in = inputs[block_id * TOK_DEV:(block_id + 1) * TOK_DEV].astype(jnp.float32)
        rows_grad = out_grad[block_id * TOK_DEV:(block_id + 1) * TOK_DEV].astype(jnp.float32)
        total = total + rounded(jnp.dot(rows_in.T, rows_grad, precision=lax.Precision.HIGHEST))
    factor = float(TOKENS) ** (-0.5)
    return (total * factor).astype(jnp.bfloat16)

def reference(attn_values, attn_exponents, hidden_values, hidden_exponents, attn_out_grad, mlp_out_grad, attn_weight, mlp_weight):
    attn_inputs = dequantize(attn_values, attn_exponents)
    hidden_inputs = dequantize(hidden_values, hidden_exponents)
    attn_input_grad = input_grad(attn_out_grad, attn_weight)
    mlp_input_grad = input_grad(mlp_out_grad, mlp_weight)
    attn_weight_grad = weight_grad(attn_inputs, attn_out_grad)
    mlp_weight_grad = weight_grad(hidden_inputs, mlp_out_grad)
    return (attn_input_grad, mlp_input_grad, attn_weight_grad, mlp_weight_grad)
```

```python
import functools

import jax
import jax.numpy as jnp
from jax import lax
from jax.experimental import pallas as pl
from jax.experimental.pallas import tpu as pltpu
from jax.sharding import PartitionSpec as P

BLOCK = 128
N = 8
NX = 4
CHUNKS = 3
MESH = pl.DeviceIdType.MESH
F32 = jnp.float32
BF16 = jnp.bfloat16


def dequantize(values, exponents):
    tokens, width = values.shape
    scales = jnp.exp2(exponents.astype(F32))
    wide = jnp.repeat(scales, BLOCK, axis=1)
    mine = lax.dynamic_slice_in_dim(wide, lax.axis_index("gz") * width, width, axis=1)
    return (values.astype(F32) * mine).astype(BF16)


def kernel(
    factor, xt, ga, gm, wa, wm, dxt, dwa, dwm,
    wown, xf, ru, rd, p, qk, qs, qc, qp, qr, dxa,
    us, ur, ds, dr, xs, xr, cs, cr, qcs, qcr, qxs, qxr,
):
    gx, k, gz = lax.axis_index("gx"), lax.axis_index("gy"), lax.axis_index("gz")
    x, c = gz // 2, gz % 2
    sib = (gx, k, 2 * x + 1 - c)
    rows_a = wa.shape[0]
    rows = rows_a + wm.shape[0]
    step = rows // CHUNKS
    above, below = (gx, k + 1, gz), (gx, k - 1, gz)

    def chip(other):
        return (gx, k, 2 * other + c)

    barrier = pltpu.get_barrier_semaphore()

    def greet(device):
        pl.semaphore_signal(barrier, inc=1, device_id=device, device_id_type=MESH)

    greet(sib)
    for d in (1, 2, 3):
        greet(chip((x + d) % NX))
    pl.when(k < N - 1)(lambda: greet(above))
    pl.when(k > 0)(lambda: greet(below))
    pl.semaphore_wait(barrier, NX + (k < N - 1).astype(jnp.int32) + (k > 0).astype(jnp.int32))

    def remote(src, dst, send, recv, device):
        return pltpu.make_async_remote_copy(
            src_ref=src, dst_ref=dst, send_sem=send, recv_sem=recv, device_id=device, device_id_type=MESH
        )

    wown[:rows_a] = wa[...]
    wown[rows_a:] = wm[...]

    def up(s, i, src):
        at = pl.ds(i * step, step)
        index = (k - s + N) % N
        source = wown.at[at] if src is None else ru.at[index, at]
        return remote(source, ru.at[index, at], us.at[s, i], ur.at[s, i], above)

    def down(s, i, src):
        at = pl.ds(i * step, step)
        index = (k + s) % N
        source = wown.at[at] if src is None else rd.at[index, at]
        return remote(source, rd.at[index, at], ds.at[s, i], dr.at[s, i], below)

    for i in range(CHUNKS):
        pl.when(k < N - 1)(lambda: up(0, i, None).start())
        pl.when(k > 0)(lambda: down(0, i, None).start())

    def x_copy(d):
        return remote(xt, xf.at[gz], xs.at[d], xr.at[d], chip((x + d) % NX))

    def core_copy(d):
        index = 2 * ((x - d + NX) % NX) + c
        return remote(xt if d == 0 else xf.at[index], xf.at[index], cs.at[d], cr.at[d], sib)

    for d in (1, 3, 2):
        x_copy(d).start()
    core_copy(0).start()

    def grad_dot(w, j):
        dims = (((1,), (1,)), ((), ()))
        top = lax.dot_general(w[:rows_a], ga[...], dims, preferred_element_type=F32)
        low = lax.dot_general(w[rows_a:], gm[...], dims, preferred_element_type=F32)
        xj, cj = j // 2, j % 2
        qk[xj, :rows_a] = top
        qk[xj, rows_a:] = low

        @pl.when(cj != c)
        def _():
            qs[xj] = qk[xj].astype(BF16)
            remote(qs.at[xj], qc.at[xj], qcs.at[xj], qcr.at[xj], sib).start()

    def pair_sum(j):
        xj, cj = j // 2, j % 2

        @pl.when(cj == c)
        def _():
            remote(qs.at[xj], qc.at[xj], qcs.at[xj], qcr.at[xj], sib).wait_recv()

            @pl.when(xj != x)
            def _():
                qp[xj] = (qk[xj] + qc[xj].astype(F32)).astype(BF16)
                remote(qp.at[xj], qr.at[x], qxs.at[xj], qxr.at[x], chip(xj)).start()

            @pl.when(xj == x)
            def _():
                dxa[...] = qk[xj] + qc[xj].astype(F32)

    def weight_dot(source, index):
        p[index, :rows_a] = jnp.dot(source[:rows_a], ga[...], preferred_element_type=F32)
        p[index, rows_a:] = jnp.dot(source[rows_a:], gm[...], preferred_element_type=F32)

    grad_dot(wown, k)
    weight_dot(xt, gz)

    def slot(s, kinds):
        for i in range(CHUNKS):
            at = pl.ds(i * step, step)
            for buf, copy, first, last, index, weights in (
                (ru, up, k == 0, k == N - 1, (k - s + N) % N, s <= k),
                (rd, down, k == N - 1, k == 0, (k + s) % N, s <= N - 1 - k),
            ):
                if "w" in kinds:
                    @pl.when(weights)
                    def _():
                        copy(s - 1, i, 1).wait_recv()

                        @pl.when(jnp.logical_not(last))
                        def _():
                            copy(s, i, 1).start()

                if "s" in kinds:
                    @pl.when(jnp.logical_not(weights | last))
                    def _():
                        @pl.when(jnp.logical_not(first))
                        def _():
                            copy(s - 1, i, 1).wait_recv()
                            buf[index, at] = (p[index, at] + buf[index, at].astype(F32)).astype(BF16)

                        @pl.when(first)
                        def _():
                            buf[index, at] = p[index, at].astype(BF16)

                        copy(s, i, 1).start()

    def input_parts(s):
        @pl.when(k - s >= 0)
        def _():
            grad_dot(ru.at[k - s], k - s)

        @pl.when(k + s < N)
        def _():
            grad_dot(rd.at[k + s], k + s)

    def input_sums(s):
        pl.when(k - s >= 0)(lambda: pair_sum(k - s))
        pl.when(k + s < N)(lambda: pair_sum(k + s))

    slot(1, "w")
    for d in (1, 3, 2):
        x_copy(d).wait_recv()
        core_copy(d).start()
        index = 2 * ((x - d + NX) % NX) + c
        weight_dot(xf.at[index], index)
    for d in (0, 1, 3, 2):
        core_copy(d).wait_recv()
        index = 2 * ((x - d + NX) % NX) + 1 - c
        weight_dot(xf.at[index], index)
    slot(1, "s")
    pair_sum(k)
    input_parts(1)

    def body(s, carry):
        slot(s, "ws")
        input_sums(s - 1)
        input_parts(s)
        return carry

    lax.fori_loop(2, N, body, 0)
    input_sums(N - 1)

    for buf, copy, none in ((ru, up, k == 0), (rd, down, k == N - 1)):
        @pl.when(jnp.logical_not(none))
        def _():
            for i in range(CHUNKS):
                copy(N - 1, i, 1).wait_recv()
            p[k] = p[k] + buf[k].astype(F32)

    dwa[...] = (p[k, :rows_a] * factor).astype(BF16)
    dwm[...] = (p[k, rows_a:] * factor).astype(BF16)

    for d in (1, 3, 2):
        other = (x - d + NX) % NX
        remote(qp.at[other], qr.at[other], qxs.at[other], qxr.at[other], chip(other)).wait_recv()
        dxa[...] = dxa[...] + qr[other].astype(F32)
    dxt[...] = dxa[...].astype(BF16)

    for d in (1, 2, 3):
        x_copy(d).wait_send()
        other = (x + d) % NX
        remote(qp.at[other], qr.at[other], qxs.at[other], qxr.at[other], chip(other)).wait_send()
    for d in range(NX):
        core_copy(d).wait_send()
        remote(qs.at[d], qc.at[d], qcs.at[d], qcr.at[d], sib).wait_send()

    def sent(s, carry):
        for i in range(CHUNKS):
            pl.when(k < N - 1)(lambda: up(s, i, 1).wait_send())
            pl.when(k > 0)(lambda: down(s, i, 1).wait_send())
        return carry

    lax.fori_loop(0, N, sent, 0)


def on_device(
    attn_values,
    attn_exponents,
    hidden_values,
    hidden_exponents,
    attn_out_grad,
    mlp_out_grad,
    attn_weight,
    mlp_weight,
):
    tokens, width = attn_out_grad.shape
    rows_a, rows_m = attn_weight.shape[0], mlp_weight.shape[0]
    rows = rows_a + rows_m
    inputs = jnp.concatenate(
        [dequantize(attn_values, attn_exponents), dequantize(hidden_values, hidden_exponents)], axis=1
    ).T
    factor = float(tokens * N) ** (-0.5)
    vmem = pl.BlockSpec(memory_space=pltpu.VMEM)
    dma = pltpu.SemaphoreType.DMA
    dxt, dwa, dwm = pl.pallas_call(
        functools.partial(kernel, factor),
        out_shape=(
            jax.ShapeDtypeStruct((rows, tokens), BF16),
            jax.ShapeDtypeStruct((rows_a, width), BF16),
            jax.ShapeDtypeStruct((rows_m, width), BF16),
        ),
        in_specs=[vmem] * 5,
        out_specs=[vmem] * 3,
        scratch_shapes=[
            pltpu.VMEM((rows, width), BF16),
            pltpu.VMEM((N, rows, tokens), BF16),
            pltpu.VMEM((N, rows, width), BF16),
            pltpu.VMEM((N, rows, width), BF16),
            pltpu.VMEM((N, rows, width), F32),
            pltpu.VMEM((NX, rows, tokens), F32),
            pltpu.VMEM((NX, rows, tokens), BF16),
            pltpu.VMEM((NX, rows, tokens), BF16),
            pltpu.VMEM((NX, rows, tokens), BF16),
            pltpu.VMEM((NX, rows, tokens), BF16),
            pltpu.VMEM((rows, tokens), F32),
            dma((N, CHUNKS)),
            dma((N, CHUNKS)),
            dma((N, CHUNKS)),
            dma((N, CHUNKS)),
            dma((NX,)),
            dma((NX,)),
            dma((NX,)),
            dma((NX,)),
            dma((NX,)),
            dma((NX,)),
            dma((NX,)),
            dma((NX,)),
        ],
        compiler_params=pltpu.CompilerParams(
            collective_id=0, has_side_effects=True, vmem_limit_bytes=40 * 2**20
        ),
    )(inputs, attn_out_grad, mlp_out_grad, attn_weight, mlp_weight)
    grads = dxt.T
    return (grads[:, :rows_a], grads[:, rows_a:], dwa, dwm)


def solution(mesh):
    placed = (
        P("gy", ("gx", "gz")),
        P("gy", "gx"),
        P("gy", ("gx", "gz")),
        P("gy", "gx"),
        P("gy", "gz"),
        P("gy", "gz"),
        P(("gx", "gy"), "gz"),
        P(("gx", "gy"), "gz"),
    )
    return jax.shard_map(
        on_device,
        mesh=mesh,
        in_specs=placed,
        out_specs=(
            P("gy", ("gx", "gz")),
            P("gy", ("gx", "gz")),
            P(("gx", "gy"), "gz"),
            P(("gx", "gy"), "gz"),
        ),
        check_vma=False,
    )
```

```python
import functools

import jax
import jax.numpy as jnp
from jax import lax
from jax.experimental import pallas as pl
from jax.experimental.pallas import tpu as pltpu
from jax.sharding import PartitionSpec as P

BLOCK = 128
N = 8
NX = 4
CHUNKS = 6
PIECES = 3
MESH = pl.DeviceIdType.MESH
F32 = jnp.float32
BF16 = jnp.bfloat16


def when(condition, *actions):
    @pl.when(condition)
    def _():
        for action in actions:
            action()


def kernel(
    factor, xa_in, xm_in, ea_in, em_in, ga_in, gm_in, wa_in, wm_in, dxa, dxm, dwa, dwm,
    xa, xm, ea, em, ga, gm, w, xt, xf, ru, rd, p, qk, qs, qc, qp, qr, total,
    ins, us, ur, ds, dr, xs, xr, cs, cr, qcs, qcr, qxs, qxr,
):
    gx, k, gz = lax.axis_index("gx"), lax.axis_index("gy"), lax.axis_index("gz")
    x, c = gz // 2, gz % 2
    sib = (gx, k, 2 * x + 1 - c)
    rows_a, rows_m = wa_in.shape[0], wm_in.shape[0]
    rows = rows_a + rows_m
    step = rows // CHUNKS
    piece = rows // PIECES
    above, below = (gx, k + 1, gz), (gx, k - 1, gz)

    def chip(other):
        return (gx, k, 2 * other + c)

    barrier = pltpu.get_barrier_semaphore()

    def greet(device):
        pl.semaphore_signal(barrier, inc=1, device_id=device, device_id_type=MESH)

    greet(sib)
    for d in (1, 2, 3):
        greet(chip((x + d) % NX))
    when(k < N - 1, lambda: greet(above))
    when(k > 0, lambda: greet(below))

    loads = [
        pltpu.make_async_copy(src, dst, ins.at[i])
        for i, (src, dst) in enumerate(
            (
                (xa_in, xa), (ea_in, ea), (xm_in, xm), (em_in, em),
                (wa_in, w.at[pl.ds(0, rows_a)]), (wm_in, w.at[pl.ds(rows_a, rows_m)]), (ga_in, ga), (gm_in, gm),
            )
        )
    ]
    for load in loads:
        load.start()
    for load in loads[:4]:
        load.wait()

    def scaled(values, exponents, at, size, first):
        row = (gz * values.shape[0] + at) // BLOCK
        scale = jnp.exp2(exponents[pl.ds(row, 1), :].astype(F32))
        xt[first + at : first + at + size] = (values[at : at + size].astype(F32) * scale).astype(BF16)

    unit = 32
    for at in range(0, rows_a, unit):
        scaled(xa, ea, at, unit, 0)
    for at in range(0, rows_m, unit):
        scaled(xm, em, at, unit, rows_a)
    for load in loads[4:]:
        load.wait()
    pl.semaphore_wait(barrier, NX + (k < N - 1).astype(jnp.int32) + (k > 0).astype(jnp.int32))

    def remote(src, dst, send, recv, device):
        return pltpu.make_async_remote_copy(
            src_ref=src, dst_ref=dst, send_sem=send, recv_sem=recv, device_id=device, device_id_type=MESH
        )

    def up(s, i, own=False):
        at = pl.ds(i * step, step)
        index = (k - s + N) % N
        return remote(w.at[at] if own else ru.at[index, at], ru.at[index, at], us.at[s, i], ur.at[s, i], above)

    def down(s, i, own=False):
        at = pl.ds(i * step, step)
        index = (k + s) % N
        return remote(w.at[at] if own else rd.at[index, at], rd.at[index, at], ds.at[s, i], dr.at[s, i], below)

    def x_copy(d, h):
        at = pl.ds(h * piece, piece)
        return remote(xt.at[at], xf.at[gz, at], xs.at[d, h], xr.at[d, h], chip((x + d) % NX))

    def core_copy(d, h):
        at = pl.ds(h * piece, piece)
        index = 2 * ((x - d + NX) % NX) + c
        source = xt.at[at] if d == 0 else xf.at[index, at]
        return remote(source, xf.at[index, at], cs.at[d, h], cr.at[d, h], sib)

    for i in range(CHUNKS):
        when(k < N - 1, lambda: up(0, i, True).start())
        when(k > 0, lambda: down(0, i, True).start())
        if i < PIECES:
            for d in (1, 3, 2):
                x_copy(d, i).start()
            core_copy(0, i).start()
    xf[gz] = xt[...]

    def grad_dot(source, j):
        dims = (((1,), (1,)), ((), ()))
        top = lax.dot_general(source[:rows_a], ga[...], dims, preferred_element_type=F32)
        low = lax.dot_general(source[rows_a:], gm[...], dims, preferred_element_type=F32)
        xj, cj = j // 2, j % 2
        qk[xj, :rows_a] = top
        qk[xj, rows_a:] = low

        @pl.when(cj != c)
        def _():
            qs[xj] = qk[xj].astype(BF16)
            remote(qs.at[xj], qc.at[xj], qcs.at[xj], qcr.at[xj], sib).start()

    def pair_sum(j):
        xj, cj = j // 2, j % 2

        @pl.when(cj == c)
        def _():
            remote(qs.at[xj], qc.at[xj], qcs.at[xj], qcr.at[xj], sib).wait_recv()

            @pl.when(xj != x)
            def _():
                qp[xj] = (qk[xj] + qc[xj].astype(F32)).astype(BF16)
                remote(qp.at[xj], qr.at[x], qxs.at[xj], qxr.at[x], chip(xj)).start()

            @pl.when(xj == x)
            def _():
                total[...] = qk[xj] + qc[xj].astype(F32)

    def weight_dot(index, lo, hi):
        if lo < rows_a:
            p[index, lo:rows_a] = jnp.dot(xf[index, lo:rows_a], ga[...], preferred_element_type=F32)
            lo = rows_a
        p[index, lo:hi] = jnp.dot(xf[index, lo:hi], gm[...], preferred_element_type=F32)

    def sides(s):
        return (
            (ru, up, k == 0, k == N - 1, (k - s + N) % N, s <= k),
            (rd, down, k == N - 1, k == 0, (k + s) % N, s <= N - 1 - k),
        )

    def forward(s, i, kinds="ws"):
        at = pl.ds(i * step, step)
        for buf, copy, first, last, index, weights in sides(s):
            if "w" in kinds:
                @pl.when(weights)
                def _():
                    copy(s - 1, i).wait_recv()
                    when(jnp.logical_not(last), lambda: copy(s, i).start())

            if "s" in kinds:
                @pl.when(jnp.logical_not(weights | last))
                def _():
                    @pl.when(jnp.logical_not(first))
                    def _():
                        copy(s - 1, i).wait_recv()
                        buf[index, at] = (p[index, at] + buf[index, at].astype(F32)).astype(BF16)

                    @pl.when(first)
                    def _():
                        buf[index, at] = p[index, at].astype(BF16)

                    copy(s, i).start()

    def input_part(s, side):
        j = k - s if side == 0 else k + s
        when((j >= 0) & (j < N), lambda: grad_dot((ru, rd)[side].at[j], j))

    def input_sums(s):
        for j in (k - s, k + s):
            when((j >= 0) & (j < N), lambda: pair_sum(j))

    def next_partial(s, side, lo=0, hi=rows):
        _, _, _, last, index, weights = sides(s)[side]
        when(jnp.logical_not(weights | last), lambda: weight_dot(index, lo, hi))

    def x_wait(h):
        for d in (1, 3, 2):
            x_copy(d, h).wait_recv()
            core_copy(d, h).start()

    def core_wait(h):
        for d in (0, 1, 3, 2):
            core_copy(d, h).wait_recv()
        for side in range(2):
            next_partial(1, side, h * piece, (h + 1) * piece)
        for i in range(h * CHUNKS // PIECES, (h + 1) * CHUNKS // PIECES):
            forward(1, i, "s")

    grad_dot(w, k)
    for i in range(3):
        forward(1, i, "w")
    x_wait(0)
    for i in range(3, 5):
        forward(1, i, "w")
    core_wait(0)
    forward(1, 5, "w")
    x_wait(1)
    core_wait(1)
    pair_sum(k)
    x_wait(2)
    core_wait(2)
    for side in range(2):
        next_partial(2, side)

    def body(s, carry):
        forward(s, 0)
        input_part(s - 1, 0)
        forward(s, 1)
        input_part(s - 1, 1)
        forward(s, 2)
        next_partial(s + 1, 0)
        forward(s, 3)
        next_partial(s + 1, 1)
        forward(s, 4)
        input_sums(s - 1)
        forward(s, 5)
        return carry

    lax.fori_loop(2, N, body, 0)
    for side in range(2):
        input_part(N - 1, side)
    weight_dot(k, 0, rows)
    input_sums(N - 1)
    for d in (1, 3, 2):
        other = (x - d + NX) % NX
        remote(qp.at[other], qr.at[other], qxs.at[other], qxr.at[other], chip(other)).wait_recv()
        total[...] = total[...] + qr[other].astype(F32)
    dxa[...] = total[:rows_a].astype(BF16)
    dxm[...] = total[rows_a:].astype(BF16)

    for i in range(CHUNKS):
        at = pl.ds(i * step, step)
        for buf, copy, none in ((ru, up, k == 0), (rd, down, k == N - 1)):
            @pl.when(jnp.logical_not(none))
            def _():
                copy(N - 1, i).wait_recv()
                p[k, at] = p[k, at] + buf[k, at].astype(F32)

    dwa[...] = (p[k, :rows_a] * factor).astype(BF16)
    dwm[...] = (p[k, rows_a:] * factor).astype(BF16)

    for d in (1, 2, 3):
        for h in range(PIECES):
            x_copy(d, h).wait_send()
        other = (x + d) % NX
        remote(qp.at[other], qr.at[other], qxs.at[other], qxr.at[other], chip(other)).wait_send()
    for d in range(NX):
        for h in range(PIECES):
            core_copy(d, h).wait_send()
        remote(qs.at[d], qc.at[d], qcs.at[d], qcr.at[d], sib).wait_send()

    def sent(s, carry):
        for i in range(CHUNKS):
            when(k < N - 1, lambda: up(s, i).wait_send())
            when(k > 0, lambda: down(s, i).wait_send())
        return carry

    lax.fori_loop(0, N, sent, 0)


def write_out(*refs):
    n = len(refs) // 2
    sems = refs[-1]
    copies = [pltpu.make_async_copy(refs[i], refs[n + i], sems.at[i]) for i in range(n)]
    for copy in copies:
        copy.start()
    for copy in copies:
        copy.wait()


def on_device(
    attn_values,
    attn_exponents,
    hidden_values,
    hidden_exponents,
    attn_out_grad,
    mlp_out_grad,
    attn_weight,
    mlp_weight,
):
    tokens, width = attn_out_grad.shape
    rows_a, rows_m = attn_weight.shape[0], mlp_weight.shape[0]
    rows = rows_a + rows_m
    factor = float(tokens * N) ** (-0.5)
    vmem = pl.BlockSpec(memory_space=pltpu.VMEM)
    hbm = pl.BlockSpec(memory_space=pl.ANY)
    dma = pltpu.SemaphoreType.DMA
    inputs = (
        attn_values.T,
        hidden_values.T,
        attn_exponents.T,
        hidden_exponents.T,
        attn_out_grad,
        mlp_out_grad,
        attn_weight,
        mlp_weight,
    )
    shapes = (
        jax.ShapeDtypeStruct((rows_a, tokens), BF16),
        jax.ShapeDtypeStruct((rows_m, tokens), BF16),
        jax.ShapeDtypeStruct((rows_a, width), BF16),
        jax.ShapeDtypeStruct((rows_m, width), BF16),
    )
    results = pl.pallas_call(
        functools.partial(kernel, factor),
        out_shape=shapes,
        in_specs=[hbm] * 8,
        out_specs=[vmem] * 4,
        scratch_shapes=[
            *[pltpu.VMEM(a.shape, a.dtype) for a in inputs[:6]],
            pltpu.VMEM((rows, width), BF16),
            pltpu.VMEM((rows, tokens), BF16),
            pltpu.VMEM((N, rows, tokens), BF16),
            pltpu.VMEM((N, rows, width), BF16),
            pltpu.VMEM((N, rows, width), BF16),
            pltpu.VMEM((N, rows, width), F32),
            pltpu.VMEM((NX, rows, tokens), F32),
            *[pltpu.VMEM((NX, rows, tokens), BF16)] * 4,
            pltpu.VMEM((rows, tokens), F32),
            dma((8,)),
            *[dma((N, CHUNKS))] * 4,
            *[dma((NX, PIECES))] * 4,
            *[dma((NX,))] * 4,
        ],
        compiler_params=pltpu.CompilerParams(
            collective_id=0, has_side_effects=True, vmem_limit_bytes=56 * 2**20
        ),
    )(*inputs)
    dxa, dxm, dwa, dwm = pl.pallas_call(
        write_out,
        out_shape=shapes,
        in_specs=[vmem] * 4,
        out_specs=[hbm] * 4,
        scratch_shapes=[dma((4,))],
    )(*results)
    return (dxa.T, dxm.T, dwa, dwm)


def solution(mesh):
    placed = (
        P("gy", ("gx", "gz")),
        P("gy", "gx"),
        P("gy", ("gx", "gz")),
        P("gy", "gx"),
        P("gy", "gz"),
        P("gy", "gz"),
        P(("gx", "gy"), "gz"),
        P(("gx", "gy"), "gz"),
    )
    return jax.shard_map(
        on_device,
        mesh=mesh,
        in_specs=placed,
        out_specs=(
            P("gy", ("gx", "gz")),
            P("gy", ("gx", "gz")),
            P(("gx", "gy"), "gz"),
            P(("gx", "gy"), "gz"),
        ),
        check_vma=False,
    )
```

```python
import functools

import jax
import jax.numpy as jnp
from jax import lax
from jax.experimental import pallas as pl
from jax.experimental.pallas import tpu as pltpu
from jax.sharding import PartitionSpec as P

BLOCK = 128
N = 8
NX = 4
CHUNKS = 6
PIECES = 3
MESH = pl.DeviceIdType.MESH
F32 = jnp.float32
BF16 = jnp.bfloat16


def when(condition, *actions):
    @pl.when(condition)
    def _():
        for action in actions:
            action()


def kernel(
    factor, xa_in, xm_in, ea_in, em_in, ga_in, gm_in, wa_in, wm_in, dxa, dxm, dwa, dwm,
    xa, xm, ea, em, ga, gm, w, xt, xf, ru, rd, p, qk, qs, qc, qp, qr, total,
    ins, us, ur, ds, dr, xs, xr, cs, cr, qcs, qcr, qxs, qxr,
):
    gx, k, gz = lax.axis_index("gx"), lax.axis_index("gy"), lax.axis_index("gz")
    x, c = gz // 2, gz % 2
    sib = (gx, k, 2 * x + 1 - c)
    rows_a, rows_m = wa_in.shape[0], wm_in.shape[0]
    rows = rows_a + rows_m
    step = rows // CHUNKS
    piece = rows // PIECES
    above, below = (gx, k + 1, gz), (gx, k - 1, gz)

    def chip(other):
        return (gx, k, 2 * other + c)

    barrier = pltpu.get_barrier_semaphore()

    def greet(device):
        pl.semaphore_signal(barrier, inc=1, device_id=device, device_id_type=MESH)

    greet(sib)
    for d in (1, 2, 3):
        greet(chip((x + d) % NX))
    when(k < N - 1, lambda: greet(above))
    when(k > 0, lambda: greet(below))

    loads = [
        pltpu.make_async_copy(src, dst, ins.at[i])
        for i, (src, dst) in enumerate(
            (
                (wa_in, w.at[pl.ds(0, rows_a)]), (wm_in, w.at[pl.ds(rows_a, rows_m)]),
                (xa_in, xa), (ea_in, ea), (xm_in, xm), (em_in, em), (ga_in, ga), (gm_in, gm),
            )
        )
    ]
    for load in loads:
        load.start()
    for load in loads[:2]:
        load.wait()
    pl.semaphore_wait(barrier, NX + (k < N - 1).astype(jnp.int32) + (k > 0).astype(jnp.int32))

    def remote(src, dst, send, recv, device):
        return pltpu.make_async_remote_copy(
            src_ref=src, dst_ref=dst, send_sem=send, recv_sem=recv, device_id=device, device_id_type=MESH
        )

    def up(s, i, own=False):
        at = pl.ds(i * step, step)
        index = (k - s + N) % N
        return remote(w.at[at] if own else ru.at[index, at], ru.at[index, at], us.at[s, i], ur.at[s, i], above)

    def down(s, i, own=False):
        at = pl.ds(i * step, step)
        index = (k + s) % N
        return remote(w.at[at] if own else rd.at[index, at], rd.at[index, at], ds.at[s, i], dr.at[s, i], below)

    def x_copy(d, h):
        at = pl.ds(h * piece, piece)
        return remote(xt.at[at], xf.at[gz, at], xs.at[d, h], xr.at[d, h], chip((x + d) % NX))

    def core_copy(d, h):
        at = pl.ds(h * piece, piece)
        index = 2 * ((x - d + NX) % NX) + c
        source = xt.at[at] if d == 0 else xf.at[index, at]
        return remote(source, xf.at[index, at], cs.at[d, h], cr.at[d, h], sib)

    def remote_pass(d, h):
        at = pl.ds(h * piece, piece)
        index = 2 * ((x - d + NX) % NX) + c
        return remote(xf.at[index, at], xf.at[index, at], cs.at[d, h], cr.at[d, h], sib)

    for i in range(CHUNKS):
        when(k < N - 1, lambda: up(0, i, True).start())
        when(k > 0, lambda: down(0, i, True).start())

    for load in loads[2:6]:
        load.wait()

    def scaled(values, exponents, at, size, first):
        row = (gz * values.shape[0] + at) // BLOCK
        scale = jnp.exp2(exponents[pl.ds(row, 1), :].astype(F32))
        xt[first + at : first + at + size] = (values[at : at + size].astype(F32) * scale).astype(BF16)

    unit = 32
    for at in range(0, rows_a, unit):
        scaled(xa, ea, at, unit, 0)
    for at in range(0, rows_m, unit):
        scaled(xm, em, at, unit, rows_a)

    ahead = jnp.where(k < N // 2, NX - 1, 0)
    held = ((k == 0) | (k == N - 1)) & (x != ahead)

    def x_start():
        for h in range(PIECES):
            for d in (1, 3, 2):
                x_copy(d, h).start()

    when(jnp.logical_not(held), x_start)
    for h in range(PIECES):
        core_copy(0, h).start()
    xf[gz] = xt[...]
    for load in loads[6:]:
        load.wait()

    def to_core(xj, h):
        at = pl.ds(h * piece, piece)
        return remote(qs.at[xj, at], qc.at[xj, at], qcs.at[xj, h], qcr.at[xj, h], sib)

    def to_chip(xj, h, sender):
        at = pl.ds(h * piece, piece)
        return remote(qp.at[xj, at], qr.at[sender, at], qxs.at[xj, h], qxr.at[sender, h], chip(xj))

    def grad_dot(source, j, pieces=range(PIECES)):
        dims = (((1,), (1,)), ((), ()))
        xj, cj = j // 2, j % 2
        lo, hi = pieces[0] * piece, (pieces[-1] + 1) * piece
        cut = min(max(lo, rows_a), hi)
        for first, end, grads in ((lo, cut, ga), (cut, hi, gm)):
            if first < end:
                part = lax.dot_general(source[first:end], grads[...], dims, preferred_element_type=F32)

                @pl.when(cj == c)
                def _():
                    qk[xj, first:end] = part

                @pl.when(cj != c)
                def _():
                    qs[xj, first:end] = part.astype(BF16)

        @pl.when(cj != c)
        def _():
            for h in pieces:
                to_core(xj, h).start()

    def pair_sum(j, pieces=range(PIECES)):
        xj, cj = j // 2, j % 2

        @pl.when(cj == c)
        def _():
            for h in pieces:
                lo, hi = h * piece, (h + 1) * piece
                to_core(xj, h).wait_recv()

                @pl.when(xj != x)
                def _():
                    qp[xj, lo:hi] = (qk[xj, lo:hi] + qc[xj, lo:hi].astype(F32)).astype(BF16)
                    to_chip(xj, h, x).start()

                @pl.when(xj == x)
                def _():
                    total[lo:hi] = qk[xj, lo:hi] + qc[xj, lo:hi].astype(F32)

    def weight_dot(index, lo, hi):
        if lo < rows_a:
            p[index, lo:rows_a] = jnp.dot(xf[index, lo:rows_a], ga[...], preferred_element_type=F32)
            lo = rows_a
        p[index, lo:hi] = jnp.dot(xf[index, lo:hi], gm[...], preferred_element_type=F32)

    def sides(s):
        return (
            (ru, up, k == 0, k == N - 1, (k - s + N) % N, s <= k),
            (rd, down, k == N - 1, k == 0, (k + s) % N, s <= N - 1 - k),
        )

    def forward(s, i, kinds="ws"):
        at = pl.ds(i * step, step)
        for buf, copy, first, last, index, weights in sides(s):
            if "w" in kinds:
                @pl.when(weights)
                def _():
                    copy(s - 1, i).wait_recv()
                    when(jnp.logical_not(last), lambda: copy(s, i).start())

            if "s" in kinds:
                @pl.when(jnp.logical_not(weights | last))
                def _():
                    @pl.when(jnp.logical_not(first))
                    def _():
                        copy(s - 1, i).wait_recv()
                        buf[index, at] = (p[index, at] + buf[index, at].astype(F32)).astype(BF16)

                    @pl.when(first)
                    def _():
                        buf[index, at] = p[index, at].astype(BF16)

                    copy(s, i).start()

    def input_part(s, side, pieces=range(PIECES)):
        j = k - s if side == 0 else k + s
        when((j >= 0) & (j < N), lambda: grad_dot((ru, rd)[side].at[j], j, pieces))

    def input_sums(s, pieces=range(PIECES)):
        for j in (k - s, k + s):
            when((j >= 0) & (j < N), lambda: pair_sum(j, pieces))

    def next_partial(s, side, lo=0, hi=rows):
        _, _, _, last, index, weights = sides(s)[side]
        when(jnp.logical_not(weights | last), lambda: weight_dot(index, lo, hi))

    def x_wait(n, h):
        d = (x - jnp.where(k < N // 2, NX - 1 - n, n) + NX) % NX

        @pl.when(d != 0)
        def _():
            x_copy(d, h).wait_recv()
            remote_pass(d, h).start()

    def core_wait(n, h):
        d = (x - jnp.where(k < N // 2, NX - 1 - n, n) + NX) % NX
        remote_pass(d, h).wait_recv()

    def first_sums(h):
        for side in range(2):
            next_partial(1, side, h * piece, (h + 1) * piece)
        for i in range(h * CHUNKS // PIECES, (h + 1) * CHUNKS // PIECES):
            forward(1, i, "s")

    grad_dot(w, k)
    for i in range(2):
        forward(1, i, "w")
    x_wait(0, 0)
    when(held, x_start)
    forward(1, 2, "w")
    core_wait(0, 0)
    first_sums(0)
    forward(1, 3, "w")
    x_wait(0, 1)
    forward(1, 4, "w")
    core_wait(0, 1)
    first_sums(1)
    forward(1, 5, "w")
    x_wait(0, 2)
    pair_sum(k)
    core_wait(0, 2)
    first_sums(2)
    for side in range(2):
        next_partial(2, side)

    forward(2, 0)
    for h in range(PIECES):
        x_wait(1, h)
    forward(2, 1)
    for h in range(PIECES):
        core_wait(1, h)
    input_part(1, 0)
    forward(2, 2)
    for h in range(PIECES):
        x_wait(2, h)
    input_part(1, 1)
    forward(2, 3)
    for h in range(PIECES):
        x_wait(3, h)
    next_partial(3, 0)
    forward(2, 4)
    next_partial(3, 1)
    forward(2, 5)
    for n in (2, 3):
        for h in range(PIECES):
            core_wait(n, h)
    input_sums(1)

    def gone(s, i):
        when(k < N - 1, lambda: up(s, i).wait_send())
        when(k > 0, lambda: down(s, i).wait_send())

    def body(s, carry):
        forward(s, 0)
        input_part(s - 1, 0)
        gone(s - 3, 0)
        forward(s, 1)
        input_part(s - 1, 1)
        gone(s - 3, 1)
        forward(s, 2)
        next_partial(s + 1, 0)
        gone(s - 3, 2)
        forward(s, 3)
        next_partial(s + 1, 1)
        gone(s - 3, 3)
        forward(s, 4)
        input_sums(s - 1)
        gone(s - 3, 4)
        forward(s, 5)
        gone(s - 3, 5)
        return carry

    lax.fori_loop(3, N - 2, body, 0)

    for s in (N - 2, N - 1):
        for h in range(PIECES):
            for i in range(h * CHUNKS // PIECES, (h + 1) * CHUNKS // PIECES):
                forward(s, i)
                gone(s - 3, i)
            for side in range(2):
                input_part(s, side, (h,))
                if s == N - 2:
                    next_partial(s + 1, side, h * piece, (h + 1) * piece)
            if s == N - 2 and h < 2:
                input_part(s - 1, h)
            if h > 0:
                input_sums(s, (h - 1,))
        if s == N - 2:
            input_sums(s - 1)
        input_sums(s, (PIECES - 1,))
    weight_dot(k, 0, rows)
    for d in (1, 2, 3):
        for h in range(PIECES):
            x_copy(d, h).wait_send()
    for d in range(NX):
        for h in range(PIECES):
            core_copy(d, h).wait_send()
    for s in (N - 3, N - 2):
        for i in range(CHUNKS):
            gone(s, i)

    def last_sums():
        for d in (1, 3, 2):
            other = (x - d + NX) % NX
            for h in range(PIECES):
                to_chip(other, h, other).wait_recv()
            total[...] = total[...] + qr[other].astype(F32)
        dxa[...] = total[:rows_a].astype(BF16)
        dxm[...] = total[rows_a:].astype(BF16)

    def last_rows():
        for i in range(CHUNKS):
            lo, hi = i * step, (i + 1) * step
            for buf, copy, none in ((ru, up, k == 0), (rd, down, k == N - 1)):
                @pl.when(jnp.logical_not(none))
                def _():
                    copy(N - 1, i).wait_recv()
                    p[k, lo:hi] = p[k, lo:hi] + buf[k, lo:hi].astype(F32)

            cut = min(max(lo, rows_a), hi)
            if lo < cut:
                dwa[lo:cut] = (p[k, lo:cut] * factor).astype(BF16)
            if cut < hi:
                dwm[cut - rows_a : hi - rows_a] = (p[k, cut:hi] * factor).astype(BF16)

    last_rows()
    last_sums()
    for d in (1, 2, 3):
        for h in range(PIECES):
            to_chip((x + d) % NX, h, x).wait_send()
    for d in range(NX):
        for h in range(PIECES):
            to_core(d, h).wait_send()
    for i in range(CHUNKS):
        gone(N - 1, i)


def write_out(*refs):
    n = len(refs) // 2
    sems = refs[-1]
    copies = [pltpu.make_async_copy(refs[i], refs[n + i], sems.at[i]) for i in range(n)]
    for copy in copies:
        copy.start()
    for copy in copies:
        copy.wait()


def on_device(
    attn_values,
    attn_exponents,
    hidden_values,
    hidden_exponents,
    attn_out_grad,
    mlp_out_grad,
    attn_weight,
    mlp_weight,
):
    tokens, width = attn_out_grad.shape
    rows_a, rows_m = attn_weight.shape[0], mlp_weight.shape[0]
    rows = rows_a + rows_m
    factor = float(tokens * N) ** (-0.5)
    vmem = pl.BlockSpec(memory_space=pltpu.VMEM)
    hbm = pl.BlockSpec(memory_space=pl.ANY)
    dma = pltpu.SemaphoreType.DMA
    inputs = (
        attn_values.T,
        hidden_values.T,
        attn_exponents.T,
        hidden_exponents.T,
        attn_out_grad,
        mlp_out_grad,
        attn_weight,
        mlp_weight,
    )
    shapes = (
        jax.ShapeDtypeStruct((rows_a, tokens), BF16),
        jax.ShapeDtypeStruct((rows_m, tokens), BF16),
        jax.ShapeDtypeStruct((rows_a, width), BF16),
        jax.ShapeDtypeStruct((rows_m, width), BF16),
    )
    results = pl.pallas_call(
        functools.partial(kernel, factor),
        out_shape=shapes,
        in_specs=[hbm] * 8,
        out_specs=[vmem] * 4,
        scratch_shapes=[
            *[pltpu.VMEM(a.shape, a.dtype) for a in inputs[:6]],
            pltpu.VMEM((rows, width), BF16),
            pltpu.VMEM((rows, tokens), BF16),
            pltpu.VMEM((N, rows, tokens), BF16),
            pltpu.VMEM((N, rows, width), BF16),
            pltpu.VMEM((N, rows, width), BF16),
            pltpu.VMEM((N, rows, width), F32),
            pltpu.VMEM((NX, rows, tokens), F32),
            *[pltpu.VMEM((NX, rows, tokens), BF16)] * 4,
            pltpu.VMEM((rows, tokens), F32),
            dma((8,)),
            *[dma((N, CHUNKS))] * 4,
            *[dma((NX, PIECES))] * 8,
        ],
        compiler_params=pltpu.CompilerParams(
            collective_id=0, has_side_effects=True, vmem_limit_bytes=56 * 2**20
        ),
    )(*inputs)
    dxa, dxm, dwa, dwm = pl.pallas_call(
        write_out,
        out_shape=shapes,
        in_specs=[vmem] * 4,
        out_specs=[hbm] * 4,
        scratch_shapes=[dma((4,))],
    )(*results)
    return (dxa.T, dxm.T, dwa, dwm)


def solution(mesh):
    placed = (
        P("gy", ("gx", "gz")),
        P("gy", "gx"),
        P("gy", ("gx", "gz")),
        P("gy", "gx"),
        P("gy", "gz"),
        P("gy", "gz"),
        P(("gx", "gy"), "gz"),
        P(("gx", "gy"), "gz"),
    )
    return jax.shard_map(
        on_device,
        mesh=mesh,
        in_specs=placed,
        out_specs=(
            P("gy", ("gx", "gz")),
            P("gy", ("gx", "gz")),
            P(("gx", "gy"), "gz"),
            P(("gx", "gy"), "gz"),
        ),
        check_vma=False,
    )
```

```python
import functools

import jax
import jax.numpy as jnp
from jax import lax
from jax.experimental import pallas as pl
from jax.experimental.pallas import tpu as pltpu
from jax.sharding import PartitionSpec as P

BLOCK = 128
N = 8
NX = 4
CHUNKS = 3
PIECES = 3
MESH = pl.DeviceIdType.MESH
F32 = jnp.float32
BF16 = jnp.bfloat16


def when(condition, *actions):
    @pl.when(condition)
    def _():
        for action in actions:
            action()


def kernel(
    factor, xa_in, xm_in, ea_in, em_in, ga_in, gm_in, wa_in, wm_in, dxa, dxm, dwa, dwm,
    xa, xm, ea, em, ga, gm, w, xt, xf, ru, rd, p, qk, qs, qc, qp, qr, total,
    ins, us, ur, ds, dr, xs, xr, cs, cr, qcs, qcr, qxs, qxr,
):
    gx, k, gz = lax.axis_index("gx"), lax.axis_index("gy"), lax.axis_index("gz")
    x, c = gz // 2, gz % 2
    sib = (gx, k, 2 * x + 1 - c)
    rows_a, rows_m = wa_in.shape[0], wm_in.shape[0]
    rows = rows_a + rows_m
    step = rows // CHUNKS
    piece = rows // PIECES
    above, below = (gx, k + 1, gz), (gx, k - 1, gz)

    def chip(other):
        return (gx, k, 2 * other + c)

    barrier = pltpu.get_barrier_semaphore()

    def greet(device):
        pl.semaphore_signal(barrier, inc=1, device_id=device, device_id_type=MESH)

    greet(sib)
    for d in (1, 2, 3):
        greet(chip((x + d) % NX))
    when(k < N - 1, lambda: greet(above))
    when(k > 0, lambda: greet(below))

    loads = [
        pltpu.make_async_copy(src, dst, ins.at[i])
        for i, (src, dst) in enumerate(
            (
                (wa_in, w.at[pl.ds(0, rows_a)]), (wm_in, w.at[pl.ds(rows_a, rows_m)]),
                (xa_in, xa), (ea_in, ea), (xm_in, xm), (em_in, em), (ga_in, ga), (gm_in, gm),
            )
        )
    ]
    for load in loads:
        load.start()
    for load in loads[:2]:
        load.wait()
    pl.semaphore_wait(barrier, NX + (k < N - 1).astype(jnp.int32) + (k > 0).astype(jnp.int32))

    def remote(src, dst, send, recv, device):
        return pltpu.make_async_remote_copy(
            src_ref=src, dst_ref=dst, send_sem=send, recv_sem=recv, device_id=device, device_id_type=MESH
        )

    def up(s, i, own=False):
        at = pl.ds(i * step, step)
        index = (k - s + N) % N
        return remote(w.at[at] if own else ru.at[index, at], ru.at[index, at], us.at[s, i], ur.at[s, i], above)

    def down(s, i, own=False):
        at = pl.ds(i * step, step)
        index = (k + s) % N
        return remote(w.at[at] if own else rd.at[index, at], rd.at[index, at], ds.at[s, i], dr.at[s, i], below)

    def x_copy(d, h):
        at = pl.ds(h * piece, piece)
        return remote(xt.at[at], xf.at[gz, at], xs.at[d, h], xr.at[d, h], chip((x + d) % NX))

    def core_copy(d, h):
        at = pl.ds(h * piece, piece)
        index = 2 * ((x - d + NX) % NX) + c
        source = xt.at[at] if d == 0 else xf.at[index, at]
        return remote(source, xf.at[index, at], cs.at[d, h], cr.at[d, h], sib)

    def remote_pass(d, h):
        at = pl.ds(h * piece, piece)
        index = 2 * ((x - d + NX) % NX) + c
        return remote(xf.at[index, at], xf.at[index, at], cs.at[d, h], cr.at[d, h], sib)

    for i in range(CHUNKS):
        when(k < N - 1, lambda: up(0, i, True).start())
        when(k > 0, lambda: down(0, i, True).start())

    for load in loads[2:6]:
        load.wait()

    def scaled(values, exponents, at, size, first):
        row = (gz * values.shape[0] + at) // BLOCK
        scale = jnp.exp2(exponents[pl.ds(row, 1), :].astype(F32))
        xt[first + at : first + at + size] = (values[at : at + size].astype(F32) * scale).astype(BF16)

    unit = 32
    for at in range(0, rows_a, unit):
        scaled(xa, ea, at, unit, 0)
    for at in range(0, rows_m, unit):
        scaled(xm, em, at, unit, rows_a)

    ahead = jnp.where(k < N // 2, NX - 1, 0)
    held = ((k == 0) | (k == N - 1)) & (x != ahead)

    def x_start():
        for h in range(PIECES):
            for d in (1, 3, 2):
                x_copy(d, h).start()

    when(jnp.logical_not(held), x_start)
    for h in range(PIECES):
        core_copy(0, h).start()
    xf[gz] = xt[...]
    for load in loads[6:]:
        load.wait()

    def to_core(xj, h):
        at = pl.ds(h * piece, piece)
        return remote(qs.at[xj, at], qc.at[xj, at], qcs.at[xj, h], qcr.at[xj, h], sib)

    def to_chip(xj, h, sender):
        at = pl.ds(h * piece, piece)
        return remote(qp.at[xj, at], qr.at[sender, at], qxs.at[xj, h], qxr.at[sender, h], chip(xj))

    def grad_dot(source, j, pieces=range(PIECES)):
        dims = (((1,), (1,)), ((), ()))
        xj, cj = j // 2, j % 2
        lo, hi = pieces[0] * piece, (pieces[-1] + 1) * piece
        cut = min(max(lo, rows_a), hi)
        for first, end, grads in ((lo, cut, ga), (cut, hi, gm)):
            if first < end:
                part = lax.dot_general(source[first:end], grads[...], dims, preferred_element_type=F32)

                @pl.when(cj == c)
                def _():
                    qk[xj, first:end] = part

                @pl.when(cj != c)
                def _():
                    qs[xj, first:end] = part.astype(BF16)

        @pl.when(cj != c)
        def _():
            for h in pieces:
                to_core(xj, h).start()

    def pair_sum(j, pieces=range(PIECES)):
        xj, cj = j // 2, j % 2

        @pl.when(cj == c)
        def _():
            for h in pieces:
                lo, hi = h * piece, (h + 1) * piece
                to_core(xj, h).wait_recv()

                @pl.when(xj != x)
                def _():
                    qp[xj, lo:hi] = (qk[xj, lo:hi] + qc[xj, lo:hi].astype(F32)).astype(BF16)
                    to_chip(xj, h, x).start()

                @pl.when(xj == x)
                def _():
                    total[lo:hi] = qk[xj, lo:hi] + qc[xj, lo:hi].astype(F32)

    def weight_dot(index, lo, hi):
        if lo < rows_a:
            p[index, lo:rows_a] = jnp.dot(xf[index, lo:rows_a], ga[...], preferred_element_type=F32)
            lo = rows_a
        p[index, lo:hi] = jnp.dot(xf[index, lo:hi], gm[...], preferred_element_type=F32)

    def sides(s):
        return (
            (ru, up, k == 0, k == N - 1, (k - s + N) % N, s <= k),
            (rd, down, k == N - 1, k == 0, (k + s) % N, s <= N - 1 - k),
        )

    def forward(s, i, kinds="ws"):
        at = pl.ds(i * step, step)
        for buf, copy, first, last, index, weights in sides(s):
            if "w" in kinds:
                @pl.when(weights)
                def _():
                    copy(s - 1, i).wait_recv()
                    when(jnp.logical_not(last), lambda: copy(s, i).start())

            if "s" in kinds:
                @pl.when(jnp.logical_not(weights | last))
                def _():
                    @pl.when(jnp.logical_not(first))
                    def _():
                        copy(s - 1, i).wait_recv()
                        buf[index, at] = (p[index, at] + buf[index, at].astype(F32)).astype(BF16)

                    @pl.when(first)
                    def _():
                        buf[index, at] = p[index, at].astype(BF16)

                    copy(s, i).start()

    def input_part(s, side, pieces=range(PIECES)):
        j = k - s if side == 0 else k + s
        when((j >= 0) & (j < N), lambda: grad_dot((ru, rd)[side].at[j], j, pieces))

    def input_sums(s, pieces=range(PIECES)):
        for j in (k - s, k + s):
            when((j >= 0) & (j < N), lambda: pair_sum(j, pieces))

    def next_partial(s, side, lo=0, hi=rows):
        _, _, _, last, index, weights = sides(s)[side]
        when(jnp.logical_not(weights | last), lambda: weight_dot(index, lo, hi))

    def x_wait(n, h):
        d = (x - jnp.where(k < N // 2, NX - 1 - n, n) + NX) % NX

        @pl.when(d != 0)
        def _():
            x_copy(d, h).wait_recv()
            remote_pass(d, h).start()

    def core_wait(n, h):
        d = (x - jnp.where(k < N // 2, NX - 1 - n, n) + NX) % NX
        remote_pass(d, h).wait_recv()

    def first_sums(h):
        for side in range(2):
            next_partial(1, side, h * piece, (h + 1) * piece)
        for i in range(h * CHUNKS // PIECES, (h + 1) * CHUNKS // PIECES):
            forward(1, i, "s")

    grad_dot(w, k)
    forward(1, 0, "w")
    x_wait(0, 0)
    when(held, x_start)
    core_wait(0, 0)
    first_sums(0)
    forward(1, 1, "w")
    x_wait(0, 1)
    core_wait(0, 1)
    first_sums(1)
    forward(1, 2, "w")
    x_wait(0, 2)
    pair_sum(k)
    core_wait(0, 2)
    first_sums(2)
    for side in range(2):
        next_partial(2, side)

    forward(2, 0)
    for h in range(PIECES):
        x_wait(1, h)
    for h in range(PIECES):
        core_wait(1, h)
    input_part(1, 0)
    forward(2, 1)
    for h in range(PIECES):
        x_wait(2, h)
    input_part(1, 1)
    for h in range(PIECES):
        x_wait(3, h)
    next_partial(3, 0)
    forward(2, 2)
    next_partial(3, 1)
    for n in (2, 3):
        for h in range(PIECES):
            core_wait(n, h)
    input_sums(1)

    def gone(s, i):
        when(k < N - 1, lambda: up(s, i).wait_send())
        when(k > 0, lambda: down(s, i).wait_send())

    def body(s, carry):
        forward(s, 0)
        input_part(s - 1, 0)
        input_part(s - 1, 1)
        gone(s - 3, 0)
        forward(s, 1)
        next_partial(s + 1, 0)
        next_partial(s + 1, 1)
        gone(s - 3, 1)
        forward(s, 2)
        input_sums(s - 1)
        gone(s - 3, 2)
        return carry

    lax.fori_loop(3, N - 2, body, 0)

    for s in (N - 2, N - 1):
        for h in range(PIECES):
            for i in range(h * CHUNKS // PIECES, (h + 1) * CHUNKS // PIECES):
                forward(s, i)
                gone(s - 3, i)
            for side in range(2):
                input_part(s, side, (h,))
                if s == N - 2:
                    next_partial(s + 1, side, h * piece, (h + 1) * piece)
            if s == N - 2 and h < 2:
                input_part(s - 1, h)
            if h > 0:
                input_sums(s, (h - 1,))
        if s == N - 2:
            input_sums(s - 1)
        input_sums(s, (PIECES - 1,))
    weight_dot(k, 0, rows)
    for d in (1, 2, 3):
        for h in range(PIECES):
            x_copy(d, h).wait_send()
    for d in range(NX):
        for h in range(PIECES):
            core_copy(d, h).wait_send()
    for s in (N - 3, N - 2):
        for i in range(CHUNKS):
            gone(s, i)

    def last_sums():
        for d in (1, 3, 2):
            other = (x - d + NX) % NX
            for h in range(PIECES):
                to_chip(other, h, other).wait_recv()
            total[...] = total[...] + qr[other].astype(F32)
        dxa[...] = total[:rows_a].astype(BF16)
        dxm[...] = total[rows_a:].astype(BF16)

    def last_rows():
        for i in range(CHUNKS):
            lo, hi = i * step, (i + 1) * step
            for buf, copy, none in ((ru, up, k == 0), (rd, down, k == N - 1)):
                @pl.when(jnp.logical_not(none))
                def _():
                    copy(N - 1, i).wait_recv()
                    p[k, lo:hi] = p[k, lo:hi] + buf[k, lo:hi].astype(F32)

            cut = min(max(lo, rows_a), hi)
            if lo < cut:
                dwa[lo:cut] = (p[k, lo:cut] * factor).astype(BF16)
            if cut < hi:
                dwm[cut - rows_a : hi - rows_a] = (p[k, cut:hi] * factor).astype(BF16)

    last_rows()
    last_sums()
    for d in (1, 2, 3):
        for h in range(PIECES):
            to_chip((x + d) % NX, h, x).wait_send()
    for d in range(NX):
        for h in range(PIECES):
            to_core(d, h).wait_send()
    for i in range(CHUNKS):
        gone(N - 1, i)


def write_out(*refs):
    n = len(refs) // 2
    sems = refs[-1]
    copies = [pltpu.make_async_copy(refs[i], refs[n + i], sems.at[i]) for i in range(n)]
    for copy in copies:
        copy.start()
    for copy in copies:
        copy.wait()


def on_device(
    attn_values,
    attn_exponents,
    hidden_values,
    hidden_exponents,
    attn_out_grad,
    mlp_out_grad,
    attn_weight,
    mlp_weight,
):
    tokens, width = attn_out_grad.shape
    rows_a, rows_m = attn_weight.shape[0], mlp_weight.shape[0]
    rows = rows_a + rows_m
    factor = float(tokens * N) ** (-0.5)
    vmem = pl.BlockSpec(memory_space=pltpu.VMEM)
    hbm = pl.BlockSpec(memory_space=pl.ANY)
    dma = pltpu.SemaphoreType.DMA
    inputs = (
        attn_values.T,
        hidden_values.T,
        attn_exponents.T,
        hidden_exponents.T,
        attn_out_grad,
        mlp_out_grad,
        attn_weight,
        mlp_weight,
    )
    shapes = (
        jax.ShapeDtypeStruct((rows_a, tokens), BF16),
        jax.ShapeDtypeStruct((rows_m, tokens), BF16),
        jax.ShapeDtypeStruct((rows_a, width), BF16),
        jax.ShapeDtypeStruct((rows_m, width), BF16),
    )
    results = pl.pallas_call(
        functools.partial(kernel, factor),
        out_shape=shapes,
        in_specs=[hbm] * 8,
        out_specs=[vmem] * 4,
        scratch_shapes=[
            *[pltpu.VMEM(a.shape, a.dtype) for a in inputs[:6]],
            pltpu.VMEM((rows, width), BF16),
            pltpu.VMEM((rows, tokens), BF16),
            pltpu.VMEM((N, rows, tokens), BF16),
            pltpu.VMEM((N, rows, width), BF16),
            pltpu.VMEM((N, rows, width), BF16),
            pltpu.VMEM((N, rows, width), F32),
            pltpu.VMEM((NX, rows, tokens), F32),
            *[pltpu.VMEM((NX, rows, tokens), BF16)] * 4,
            pltpu.VMEM((rows, tokens), F32),
            dma((8,)),
            *[dma((N, CHUNKS))] * 4,
            *[dma((NX, PIECES))] * 8,
        ],
        compiler_params=pltpu.CompilerParams(
            collective_id=0, has_side_effects=True, vmem_limit_bytes=56 * 2**20
        ),
    )(*inputs)
    dxa, dxm, dwa, dwm = pl.pallas_call(
        write_out,
        out_shape=shapes,
        in_specs=[vmem] * 4,
        out_specs=[hbm] * 4,
        scratch_shapes=[dma((4,))],
    )(*results)
    return (dxa.T, dxm.T, dwa, dwm)


def solution(mesh):
    placed = (
        P("gy", ("gx", "gz")),
        P("gy", "gx"),
        P("gy", ("gx", "gz")),
        P("gy", "gx"),
        P("gy", "gz"),
        P("gy", "gz"),
        P(("gx", "gy"), "gz"),
        P(("gx", "gy"), "gz"),
    )
    return jax.shard_map(
        on_device,
        mesh=mesh,
        in_specs=placed,
        out_specs=(
            P("gy", ("gx", "gz")),
            P("gy", ("gx", "gz")),
            P(("gx", "gy"), "gz"),
            P(("gx", "gy"), "gz"),
        ),
        check_vma=False,
    )
```

```python
import functools

import jax
import jax.numpy as jnp
from jax import lax
from jax.experimental import pallas as pl
from jax.experimental.pallas import tpu as pltpu
from jax.sharding import PartitionSpec as P

BLOCK = 128
N = 8
NX = 4
CHUNKS = 3
PIECES = 3
MESH = pl.DeviceIdType.MESH
F32 = jnp.float32
BF16 = jnp.bfloat16


def when(condition, *actions):
    @pl.when(condition)
    def _():
        for action in actions:
            action()


def kernel(
    factor, xa_in, xm_in, ea_in, em_in, ga_in, gm_in, wa_in, wm_in, dxa, dxm, dwa, dwm,
    xa, xm, ea, em, ga, gm, w, xt, xf, ru, rd, p, qk, qs, qc, qp, qr, total,
    ins, us, ur, ds, dr, xs, xr, cs, cr, qcs, qcr, qxs, qxr,
):
    gx, k, gz = lax.axis_index("gx"), lax.axis_index("gy"), lax.axis_index("gz")
    x, c = gz // 2, gz % 2
    sib = (gx, k, 2 * x + 1 - c)
    rows_a, rows_m = wa_in.shape[0], wm_in.shape[0]
    rows = rows_a + rows_m
    step = rows // CHUNKS
    piece = rows // PIECES
    above, below = (gx, k + 1, gz), (gx, k - 1, gz)

    def chip(other):
        return (gx, k, 2 * other + c)

    barrier = pltpu.get_barrier_semaphore()

    def greet(device):
        pl.semaphore_signal(barrier, inc=1, device_id=device, device_id_type=MESH)

    greet(sib)
    for d in (1, 2, 3):
        greet(chip((x + d) % NX))
    when(k < N - 1, lambda: greet(above))
    when(k > 0, lambda: greet(below))

    loads = [
        pltpu.make_async_copy(src, dst, ins.at[i])
        for i, (src, dst) in enumerate(
            (
                (xa_in, xa), (ea_in, ea), (xm_in, xm), (em_in, em), (ga_in, ga), (gm_in, gm),
                (wa_in, w.at[pl.ds(0, rows_a)]), (wm_in, w.at[pl.ds(rows_a, rows_m)]),
            )
        )
    ]
    for load in loads:
        load.start()
    pl.semaphore_wait(barrier, NX + (k < N - 1).astype(jnp.int32) + (k > 0).astype(jnp.int32))

    def remote(src, dst, send, recv, device):
        return pltpu.make_async_remote_copy(
            src_ref=src, dst_ref=dst, send_sem=send, recv_sem=recv, device_id=device, device_id_type=MESH
        )

    def up(s, i):
        at = pl.ds(i * step, step)
        index = (k - s + N) % N
        return remote(ru.at[index, at], ru.at[index, at], us.at[s, i], ur.at[s, i], above)

    def down(s, i):
        at = pl.ds(i * step, step)
        index = (k + s) % N
        return remote(rd.at[index, at], rd.at[index, at], ds.at[s, i], dr.at[s, i], below)

    def x_copy(d, h):
        at = pl.ds(h * piece, piece)
        return remote(xt.at[at], xf.at[gz, at], xs.at[d, h], xr.at[d, h], chip((x + d) % NX))

    def core_copy(d, h):
        at = pl.ds(h * piece, piece)
        index = 2 * ((x - d + NX) % NX) + c
        source = xt.at[at] if d == 0 else xf.at[index, at]
        return remote(source, xf.at[index, at], cs.at[d, h], cr.at[d, h], sib)

    def remote_pass(d, h):
        at = pl.ds(h * piece, piece)
        index = 2 * ((x - d + NX) % NX) + c
        return remote(xf.at[index, at], xf.at[index, at], cs.at[d, h], cr.at[d, h], sib)

    def first_packet(i, buf, send, recv, device):
        lo, hi = i * step, (i + 1) * step
        cut = min(max(lo, rows_a), hi)
        if lo < cut:
            src = wa_in.at[pl.ds(lo, cut - lo)]
            remote(src, buf.at[k, pl.ds(lo, cut - lo)], send.at[0, i], recv.at[0, i], device).start()
        if cut < hi:
            src = wm_in.at[pl.ds(cut - rows_a, hi - cut)]
            remote(src, buf.at[k, pl.ds(cut, hi - cut)], send.at[0, i], recv.at[0, i], device).start()

    for i in range(CHUNKS):
        when(k < N - 1, lambda: first_packet(i, ru, us, ur, above))
        when(k > 0, lambda: first_packet(i, rd, ds, dr, below))

    for load in loads[:4]:
        load.wait()

    def scaled(values, exponents, at, size, first):
        row = (gz * values.shape[0] + at) // BLOCK
        scale = jnp.exp2(exponents[pl.ds(row, 1), :].astype(F32))
        xt[first + at : first + at + size] = (values[at : at + size].astype(F32) * scale).astype(BF16)

    unit = 32
    for at in range(0, rows_a, unit):
        scaled(xa, ea, at, unit, 0)
    for at in range(0, rows_m, unit):
        scaled(xm, em, at, unit, rows_a)

    ahead = jnp.where(k < N // 2, NX - 1, 0)
    held = ((k == 0) | (k == N - 1)) & (x != ahead)

    def x_start():
        for h in range(PIECES):
            for d in (1, 3, 2):
                x_copy(d, h).start()

    when(jnp.logical_not(held), x_start)
    for h in range(PIECES):
        core_copy(0, h).start()
    xf[gz] = xt[...]
    for load in loads[4:]:
        load.wait()

    def to_core(xj, h):
        at = pl.ds(h * piece, piece)
        return remote(qs.at[xj, at], qc.at[xj, at], qcs.at[xj, h], qcr.at[xj, h], sib)

    def to_chip(xj, h, sender):
        at = pl.ds(h * piece, piece)
        return remote(qp.at[xj, at], qr.at[sender, at], qxs.at[xj, h], qxr.at[sender, h], chip(xj))

    def grad_dot(source, j, pieces=range(PIECES)):
        dims = (((1,), (1,)), ((), ()))
        xj, cj = j // 2, j % 2
        lo, hi = pieces[0] * piece, (pieces[-1] + 1) * piece
        cut = min(max(lo, rows_a), hi)
        for first, end, grads in ((lo, cut, ga), (cut, hi, gm)):
            if first < end:
                part = lax.dot_general(source[first:end], grads[...], dims, preferred_element_type=F32)

                @pl.when(cj == c)
                def _():
                    qk[xj, first:end] = part

                @pl.when(cj != c)
                def _():
                    qs[xj, first:end] = part.astype(BF16)

        @pl.when(cj != c)
        def _():
            for h in pieces:
                to_core(xj, h).start()

    def pair_sum(j, pieces=range(PIECES)):
        xj, cj = j // 2, j % 2

        @pl.when(cj == c)
        def _():
            for h in pieces:
                lo, hi = h * piece, (h + 1) * piece
                to_core(xj, h).wait_recv()

                @pl.when(xj != x)
                def _():
                    qp[xj, lo:hi] = (qk[xj, lo:hi] + qc[xj, lo:hi].astype(F32)).astype(BF16)
                    to_chip(xj, h, x).start()

                @pl.when(xj == x)
                def _():
                    total[lo:hi] = qk[xj, lo:hi] + qc[xj, lo:hi].astype(F32)

    def weight_dot(index, lo, hi):
        if lo < rows_a:
            p[index, lo:rows_a] = jnp.dot(xf[index, lo:rows_a], ga[...], preferred_element_type=F32)
            lo = rows_a
        p[index, lo:hi] = jnp.dot(xf[index, lo:hi], gm[...], preferred_element_type=F32)

    def sides(s):
        return (
            (ru, up, k == 0, k == N - 1, (k - s + N) % N, s <= k),
            (rd, down, k == N - 1, k == 0, (k + s) % N, s <= N - 1 - k),
        )

    def forward(s, i, kinds="ws"):
        at = pl.ds(i * step, step)
        for buf, copy, first, last, index, weights in sides(s):
            if "w" in kinds:
                @pl.when(weights)
                def _():
                    copy(s - 1, i).wait_recv()
                    when(jnp.logical_not(last), lambda: copy(s, i).start())

            if "s" in kinds:
                @pl.when(jnp.logical_not(weights | last))
                def _():
                    @pl.when(jnp.logical_not(first))
                    def _():
                        copy(s - 1, i).wait_recv()
                        buf[index, at] = (p[index, at] + buf[index, at].astype(F32)).astype(BF16)

                    @pl.when(first)
                    def _():
                        buf[index, at] = p[index, at].astype(BF16)

                    copy(s, i).start()

    def input_part(s, side, pieces=range(PIECES)):
        j = k - s if side == 0 else k + s
        when((j >= 0) & (j < N), lambda: grad_dot((ru, rd)[side].at[j], j, pieces))

    def input_sums(s, pieces=range(PIECES)):
        for j in (k - s, k + s):
            when((j >= 0) & (j < N), lambda: pair_sum(j, pieces))

    def next_partial(s, side, lo=0, hi=rows):
        _, _, _, last, index, weights = sides(s)[side]
        when(jnp.logical_not(weights | last), lambda: weight_dot(index, lo, hi))

    def x_wait(n, h):
        d = (x - jnp.where(k < N // 2, NX - 1 - n, n) + NX) % NX

        @pl.when(d != 0)
        def _():
            x_copy(d, h).wait_recv()
            remote_pass(d, h).start()

    def core_wait(n, h):
        d = (x - jnp.where(k < N // 2, NX - 1 - n, n) + NX) % NX
        remote_pass(d, h).wait_recv()

    def first_sums(h):
        for side in range(2):
            next_partial(1, side, h * piece, (h + 1) * piece)
        for i in range(h * CHUNKS // PIECES, (h + 1) * CHUNKS // PIECES):
            forward(1, i, "s")

    grad_dot(w, k)
    forward(1, 0, "w")
    x_wait(0, 0)
    when(held, x_start)
    core_wait(0, 0)
    first_sums(0)
    forward(1, 1, "w")
    x_wait(0, 1)
    core_wait(0, 1)
    first_sums(1)
    forward(1, 2, "w")
    x_wait(0, 2)
    core_wait(0, 2)
    first_sums(2)
    for side in range(2):
        next_partial(2, side)

    forward(2, 0)
    for h in range(PIECES):
        x_wait(1, h)
    for h in range(PIECES):
        core_wait(1, h)
    input_part(1, 0)
    forward(2, 1)
    for h in range(PIECES):
        x_wait(2, h)
    input_part(1, 1)
    for h in range(PIECES):
        x_wait(3, h)
    next_partial(3, 0)
    forward(2, 2)
    next_partial(3, 1)
    for n in (2, 3):
        for h in range(PIECES):
            core_wait(n, h)
    pair_sum(k)

    def gone(s, i):
        when(k < N - 1, lambda: up(s, i).wait_send())
        when(k > 0, lambda: down(s, i).wait_send())

    def body(s, carry):
        forward(s, 0)
        input_part(s - 1, 0)
        input_part(s - 1, 1)
        gone(s - 3, 0)
        forward(s, 1)
        next_partial(s + 1, 0)
        next_partial(s + 1, 1)
        gone(s - 3, 1)
        forward(s, 2)
        input_sums(s - 2)
        gone(s - 3, 2)
        return carry

    lax.fori_loop(3, N - 2, body, 0)

    input_sums(N - 4)
    for s in (N - 2, N - 1):
        for h in range(PIECES):
            for i in range(h * CHUNKS // PIECES, (h + 1) * CHUNKS // PIECES):
                forward(s, i)
                gone(s - 3, i)
            for side in range(2):
                input_part(s, side, (h,))
                if s == N - 2:
                    next_partial(s + 1, side, h * piece, (h + 1) * piece)
            if s == N - 2 and h < 2:
                input_part(s - 1, h)
            if h > 0:
                input_sums(s, (h - 1,))
        if s == N - 2:
            input_sums(s - 1)
        input_sums(s, (PIECES - 1,))
    weight_dot(k, 0, rows)
    for d in (1, 2, 3):
        for h in range(PIECES):
            x_copy(d, h).wait_send()
    for d in range(NX):
        for h in range(PIECES):
            core_copy(d, h).wait_send()
    for s in (N - 3, N - 2):
        for i in range(CHUNKS):
            gone(s, i)

    def last_sums():
        for d in (1, 3, 2):
            other = (x - d + NX) % NX
            for h in range(PIECES):
                to_chip(other, h, other).wait_recv()
            total[...] = total[...] + qr[other].astype(F32)
        dxa[...] = total[:rows_a].astype(BF16)
        dxm[...] = total[rows_a:].astype(BF16)

    def last_rows(start, stop):
        for i in range(start, stop):
            lo, hi = i * step, (i + 1) * step
            for buf, copy, none in ((ru, up, k == 0), (rd, down, k == N - 1)):
                @pl.when(jnp.logical_not(none))
                def _():
                    copy(N - 1, i).wait_recv()
                    p[k, lo:hi] = p[k, lo:hi] + buf[k, lo:hi].astype(F32)

            cut = min(max(lo, rows_a), hi)
            if lo < cut:
                dwa[lo:cut] = (p[k, lo:cut] * factor).astype(BF16)
            if cut < hi:
                dwm[cut - rows_a : hi - rows_a] = (p[k, cut:hi] * factor).astype(BF16)

    for d in range(NX):
        for h in range(PIECES):
            to_core(d, h).wait_send()
    last_rows(0, 2)
    last_sums()
    for d in (1, 2, 3):
        for h in range(PIECES):
            to_chip((x + d) % NX, h, x).wait_send()
    gone(N - 1, 0)
    gone(N - 1, 1)
    last_rows(2, CHUNKS)
    gone(N - 1, CHUNKS - 1)


def write_out(*refs):
    n = (len(refs) - 2) // 3
    results, outputs, staged = refs[:n], refs[n : 2 * n], refs[2 * n : 3 * n]
    came, went = refs[3 * n :]
    reads = [pltpu.make_async_copy(results[i], staged[i], came.at[i]) for i in range(n)]
    writes = [pltpu.make_async_copy(staged[i], outputs[i], went.at[i]) for i in range(n)]
    for read in reads:
        read.start()
    for read, write in zip(reads, writes):
        read.wait()
        write.start()
    for write in writes:
        write.wait()


def on_device(
    attn_values,
    attn_exponents,
    hidden_values,
    hidden_exponents,
    attn_out_grad,
    mlp_out_grad,
    attn_weight,
    mlp_weight,
):
    tokens, width = attn_out_grad.shape
    rows_a, rows_m = attn_weight.shape[0], mlp_weight.shape[0]
    rows = rows_a + rows_m
    factor = float(tokens * N) ** (-0.5)
    vmem = pl.BlockSpec(memory_space=pltpu.VMEM)
    hbm = pl.BlockSpec(memory_space=pl.ANY)
    dma = pltpu.SemaphoreType.DMA
    inputs = (
        attn_values.T,
        hidden_values.T,
        attn_exponents.T,
        hidden_exponents.T,
        attn_out_grad,
        mlp_out_grad,
        attn_weight,
        mlp_weight,
    )
    shapes = (
        jax.ShapeDtypeStruct((rows_a, tokens), BF16),
        jax.ShapeDtypeStruct((rows_m, tokens), BF16),
        jax.ShapeDtypeStruct((rows_a, width), BF16),
        jax.ShapeDtypeStruct((rows_m, width), BF16),
    )
    results = pl.pallas_call(
        functools.partial(kernel, factor),
        out_shape=shapes,
        in_specs=[hbm] * 8,
        out_specs=[vmem] * 4,
        scratch_shapes=[
            *[pltpu.VMEM(a.shape, a.dtype) for a in inputs[:6]],
            pltpu.VMEM((rows, width), BF16),
            pltpu.VMEM((rows, tokens), BF16),
            pltpu.VMEM((N, rows, tokens), BF16),
            pltpu.VMEM((N, rows, width), BF16),
            pltpu.VMEM((N, rows, width), BF16),
            pltpu.VMEM((N, rows, width), F32),
            pltpu.VMEM((NX, rows, tokens), F32),
            *[pltpu.VMEM((NX, rows, tokens), BF16)] * 4,
            pltpu.VMEM((rows, tokens), F32),
            dma((8,)),
            *[dma((N, CHUNKS))] * 4,
            *[dma((NX, PIECES))] * 8,
        ],
        compiler_params=pltpu.CompilerParams(
            collective_id=0, has_side_effects=True, vmem_limit_bytes=56 * 2**20
        ),
    )(*inputs)
    dxa, dxm, dwa, dwm = pl.pallas_call(
        write_out,
        out_shape=shapes,
        in_specs=[hbm] * 4,
        out_specs=[hbm] * 4,
        scratch_shapes=[*[pltpu.VMEM(a.shape, a.dtype) for a in shapes], dma((4,)), dma((4,))],
    )(*results)
    return (dxa.T, dxm.T, dwa, dwm)


def solution(mesh):
    placed = (
        P("gy", ("gx", "gz")),
        P("gy", "gx"),
        P("gy", ("gx", "gz")),
        P("gy", "gx"),
        P("gy", "gz"),
        P("gy", "gz"),
        P(("gx", "gy"), "gz"),
        P(("gx", "gy"), "gz"),
    )
    return jax.shard_map(
        on_device,
        mesh=mesh,
        in_specs=placed,
        out_specs=(
            P("gy", ("gx", "gz")),
            P("gy", ("gx", "gz")),
            P(("gx", "gy"), "gz"),
            P(("gx", "gy"), "gz"),
        ),
        check_vma=False,
    )
```

```python
import functools

import jax
import jax.numpy as jnp
from jax import lax
from jax.experimental import pallas as pl
from jax.experimental.pallas import tpu as pltpu
from jax.sharding import PartitionSpec as P

BLOCK = 128
N = 8
NX = 4
CHUNKS = 3
PIECES = 3
MESH = pl.DeviceIdType.MESH
F32 = jnp.float32
BF16 = jnp.bfloat16


def when(condition, *actions):
    @pl.when(condition)
    def _():
        for action in actions:
            action()


def kernel(
    factor, xa_in, xm_in, ea_in, em_in, ga_in, gm_in, wa_in, wm_in, dxa, dxm, dwa, dwm,
    xa, xm, ea, em, ga, gm, w, xt, xf, ru, rd, p, qk, qs, qc, qp, qr, total,
    ins, us, ur, ds, dr, xs, xr, cs, cr, qcs, qcr, qxs, qxr,
):
    gx, k, gz = lax.axis_index("gx"), lax.axis_index("gy"), lax.axis_index("gz")
    x, c = gz // 2, gz % 2
    sib = (gx, k, 2 * x + 1 - c)
    rows_a, rows_m = wa_in.shape[0], wm_in.shape[0]
    rows = rows_a + rows_m
    step = rows // CHUNKS
    piece = rows // PIECES
    above, below = (gx, jnp.minimum(k + 1, N - 1), gz), (gx, jnp.maximum(k - 1, 0), gz)

    def chip(other):
        return (gx, k, 2 * other + c)

    barrier = pltpu.get_barrier_semaphore()

    def greet(device):
        pl.semaphore_signal(barrier, inc=1, device_id=device, device_id_type=MESH)

    greet(sib)
    for d in (1, 2, 3):
        greet(chip((x + d) % NX))
    when(k < N - 1, lambda: greet(above))
    when(k > 0, lambda: greet(below))

    loads = [
        pltpu.make_async_copy(src, dst, ins.at[i])
        for i, (src, dst) in enumerate(
            (
                (xa_in, xa), (ea_in, ea), (xm_in, xm), (em_in, em), (ga_in, ga), (gm_in, gm),
                (wa_in, w.at[pl.ds(0, rows_a)]), (wm_in, w.at[pl.ds(rows_a, rows_m)]),
            )
        )
    ]
    for load in loads:
        load.start()
    pl.semaphore_wait(barrier, NX + (k < N - 1).astype(jnp.int32) + (k > 0).astype(jnp.int32))

    def remote(src, dst, send, recv, device):
        return pltpu.make_async_remote_copy(
            src_ref=src, dst_ref=dst, send_sem=send, recv_sem=recv, device_id=device, device_id_type=MESH
        )

    def up(s, i):
        at = pl.ds(i * step, step)
        index = (k - s + N) % N
        return remote(ru.at[index, at], ru.at[index, at], us.at[s, i], ur.at[s, i], above)

    def down(s, i):
        at = pl.ds(i * step, step)
        index = (k + s) % N
        return remote(rd.at[index, at], rd.at[index, at], ds.at[s, i], dr.at[s, i], below)

    def x_copy(d, h):
        at = pl.ds(h * piece, piece)
        return remote(xt.at[at], xf.at[gz, at], xs.at[d, h], xr.at[d, h], chip((x + d) % NX))

    def core_copy(d, h):
        at = pl.ds(h * piece, piece)
        index = 2 * ((x - d + NX) % NX) + c
        source = xt.at[at] if d == 0 else xf.at[index, at]
        return remote(source, xf.at[index, at], cs.at[d, h], cr.at[d, h], sib)

    def remote_pass(d, h):
        at = pl.ds(h * piece, piece)
        index = 2 * ((x - d + NX) % NX) + c
        return remote(xf.at[index, at], xf.at[index, at], cs.at[d, h], cr.at[d, h], sib)

    def first_packet(i, buf, send, recv, device):
        lo, hi = i * step, (i + 1) * step
        cut = min(max(lo, rows_a), hi)
        if lo < cut:
            src = wa_in.at[pl.ds(lo, cut - lo)]
            remote(src, buf.at[k, pl.ds(lo, cut - lo)], send.at[0, i], recv.at[0, i], device).start()
        if cut < hi:
            src = wm_in.at[pl.ds(cut - rows_a, hi - cut)]
            remote(src, buf.at[k, pl.ds(cut, hi - cut)], send.at[0, i], recv.at[0, i], device).start()

    for i in range(CHUNKS):
        when(k < N - 1, lambda: first_packet(i, ru, us, ur, above))
        when(k > 0, lambda: first_packet(i, rd, ds, dr, below))

    for load in loads[:4]:
        load.wait()

    def scaled(values, exponents, at, size, first):
        row = (gz * values.shape[0] + at) // BLOCK
        scale = jnp.exp2(exponents[pl.ds(row, 1), :].astype(F32))
        xt[first + at : first + at + size] = (values[at : at + size].astype(F32) * scale).astype(BF16)

    unit = 32
    for at in range(0, rows_a, unit):
        scaled(xa, ea, at, unit, 0)
    for at in range(0, rows_m, unit):
        scaled(xm, em, at, unit, rows_a)

    ahead = jnp.where(k < N // 2, NX - 1, 0)
    held = ((k == 0) | (k == N - 1)) & (x != ahead)

    def x_start():
        for h in range(PIECES):
            for d in (1, 3, 2):
                x_copy(d, h).start()

    when(jnp.logical_not(held), x_start)
    for h in range(PIECES):
        core_copy(0, h).start()
    xf[gz] = xt[...]
    for load in loads[4:]:
        load.wait()

    def to_core(xj, h):
        at = pl.ds(h * piece, piece)
        return remote(qs.at[xj, at], qc.at[xj, at], qcs.at[xj, h], qcr.at[xj, h], sib)

    def to_chip(xj, h, sender):
        at = pl.ds(h * piece, piece)
        return remote(qp.at[xj, at], qr.at[sender, at], qxs.at[xj, h], qxr.at[sender, h], chip(xj))

    def grad_dot(source, j, pieces=range(PIECES)):
        dims = (((1,), (1,)), ((), ()))
        xj, cj = j // 2, j % 2
        lo, hi = pieces[0] * piece, (pieces[-1] + 1) * piece
        cut = min(max(lo, rows_a), hi)
        for first, end, grads in ((lo, cut, ga), (cut, hi, gm)):
            if first < end:
                part = lax.dot_general(source[first:end], grads[...], dims, preferred_element_type=F32)

                @pl.when(cj == c)
                def _():
                    qk[xj, first:end] = part

                @pl.when(cj != c)
                def _():
                    qs[xj, first:end] = part.astype(BF16)

        @pl.when(cj != c)
        def _():
            for h in pieces:
                to_core(xj, h).start()

    def pair_sum(j, pieces=range(PIECES)):
        xj, cj = j // 2, j % 2

        @pl.when(cj == c)
        def _():
            for h in pieces:
                lo, hi = h * piece, (h + 1) * piece
                to_core(xj, h).wait_recv()

                @pl.when(xj != x)
                def _():
                    qp[xj, lo:hi] = (qk[xj, lo:hi] + qc[xj, lo:hi].astype(F32)).astype(BF16)
                    to_chip(xj, h, x).start()

                @pl.when(xj == x)
                def _():
                    total[lo:hi] = qk[xj, lo:hi] + qc[xj, lo:hi].astype(F32)

    def weight_dot(index, lo, hi):
        if lo < rows_a:
            p[index, lo:rows_a] = jnp.dot(xf[index, lo:rows_a], ga[...], preferred_element_type=F32)
            lo = rows_a
        p[index, lo:hi] = jnp.dot(xf[index, lo:hi], gm[...], preferred_element_type=F32)

    def sides(s):
        return (
            (ru, up, k == 0, k == N - 1, (k - s + N) % N, s <= k),
            (rd, down, k == N - 1, k == 0, (k + s) % N, s <= N - 1 - k),
        )

    def forward(s, i, kinds="ws"):
        at = pl.ds(i * step, step)
        for buf, copy, first, last, index, weights in sides(s):
            if "w" in kinds:
                @pl.when(weights)
                def _():
                    copy(s - 1, i).wait_recv()
                    when(jnp.logical_not(last), lambda: copy(s, i).start())

            if "s" in kinds:
                @pl.when(jnp.logical_not(weights | last))
                def _():
                    @pl.when(jnp.logical_not(first))
                    def _():
                        copy(s - 1, i).wait_recv()
                        buf[index, at] = (p[index, at] + buf[index, at].astype(F32)).astype(BF16)

                    @pl.when(first)
                    def _():
                        buf[index, at] = p[index, at].astype(BF16)

                    copy(s, i).start()

    def input_part(s, side, pieces=range(PIECES)):
        j = k - s if side == 0 else k + s
        when((j >= 0) & (j < N), lambda: grad_dot((ru, rd)[side].at[j], j, pieces))

    def input_sums(s, pieces=range(PIECES)):
        for j in (k - s, k + s):
            when((j >= 0) & (j < N), lambda: pair_sum(j, pieces))

    def next_partial(s, side, lo=0, hi=rows):
        _, _, _, last, index, weights = sides(s)[side]
        when(jnp.logical_not(weights | last), lambda: weight_dot(index, lo, hi))

    def x_wait(n, h):
        d = (x - jnp.where(k < N // 2, NX - 1 - n, n) + NX) % NX

        @pl.when(d != 0)
        def _():
            x_copy(d, h).wait_recv()
            remote_pass(d, h).start()

    def core_wait(n, h):
        d = (x - jnp.where(k < N // 2, NX - 1 - n, n) + NX) % NX
        remote_pass(d, h).wait_recv()

    def first_sums(h):
        for side in range(2):
            next_partial(1, side, h * piece, (h + 1) * piece)
        for i in range(h * CHUNKS // PIECES, (h + 1) * CHUNKS // PIECES):
            forward(1, i, "s")

    grad_dot(w, k)
    forward(1, 0, "w")
    x_wait(0, 0)
    when(held, x_start)
    core_wait(0, 0)
    first_sums(0)
    forward(1, 1, "w")
    x_wait(0, 1)
    core_wait(0, 1)
    first_sums(1)
    forward(1, 2, "w")
    x_wait(0, 2)
    core_wait(0, 2)
    first_sums(2)
    for side in range(2):
        next_partial(2, side)

    forward(2, 0)
    for h in range(PIECES):
        x_wait(1, h)
    for h in range(PIECES):
        core_wait(1, h)
    input_part(1, 0)
    forward(2, 1)
    for h in range(PIECES):
        x_wait(2, h)
    input_part(1, 1)
    for h in range(PIECES):
        x_wait(3, h)
    next_partial(3, 0)
    forward(2, 2)
    next_partial(3, 1)
    for n in (2, 3):
        for h in range(PIECES):
            core_wait(n, h)
    pair_sum(k)

    def gone(s, i):
        when(k < N - 1, lambda: up(s, i).wait_send())
        when(k > 0, lambda: down(s, i).wait_send())

    def body(s, carry):
        forward(s, 0)
        input_part(s - 1, 0)
        input_part(s - 1, 1)
        gone(s - 3, 0)
        forward(s, 1)
        next_partial(s + 1, 0)
        next_partial(s + 1, 1)
        gone(s - 3, 1)
        forward(s, 2)
        input_sums(s - 2)
        gone(s - 3, 2)
        return carry

    lax.fori_loop(3, N - 2, body, 0)

    input_sums(N - 4)
    for s in (N - 2, N - 1):
        for h in range(PIECES):
            for i in range(h * CHUNKS // PIECES, (h + 1) * CHUNKS // PIECES):
                forward(s, i)
                gone(s - 3, i)
            for side in range(2):
                input_part(s, side, (h,))
                if s == N - 2:
                    next_partial(s + 1, side, h * piece, (h + 1) * piece)
            if s == N - 2 and h < 2:
                input_part(s - 1, h)
            if h > 0:
                input_sums(s, (h - 1,))
        if s == N - 2:
            input_sums(s - 1)
        input_sums(s, (PIECES - 1,))
    weight_dot(k, 0, rows)
    for d in (1, 2, 3):
        for h in range(PIECES):
            x_copy(d, h).wait_send()
    for d in range(NX):
        for h in range(PIECES):
            core_copy(d, h).wait_send()
    for s in (N - 3, N - 2):
        for i in range(CHUNKS):
            gone(s, i)

    def last_sums():
        for d in (1, 3, 2):
            other = (x - d + NX) % NX
            for h in range(PIECES):
                to_chip(other, h, other).wait_recv()
            total[...] = total[...] + qr[other].astype(F32)
        dxa[...] = total[:rows_a].astype(BF16)
        dxm[...] = total[rows_a:].astype(BF16)

    def last_rows(start, stop):
        for i in range(start, stop):
            lo, hi = i * step, (i + 1) * step
            for buf, copy, none in ((ru, up, k == 0), (rd, down, k == N - 1)):
                @pl.when(jnp.logical_not(none))
                def _():
                    copy(N - 1, i).wait_recv()
                    p[k, lo:hi] = p[k, lo:hi] + buf[k, lo:hi].astype(F32)

            cut = min(max(lo, rows_a), hi)
            if lo < cut:
                dwa[lo:cut] = (p[k, lo:cut] * factor).astype(BF16)
            if cut < hi:
                dwm[cut - rows_a : hi - rows_a] = (p[k, cut:hi] * factor).astype(BF16)

    for d in range(NX):
        for h in range(PIECES):
            to_core(d, h).wait_send()
    last_rows(0, 2)
    last_sums()
    for d in (1, 2, 3):
        for h in range(PIECES):
            to_chip((x + d) % NX, h, x).wait_send()
    gone(N - 1, 0)
    gone(N - 1, 1)
    last_rows(2, CHUNKS)
    gone(N - 1, CHUNKS - 1)


def write_out(*refs):
    n = (len(refs) - 2) // 3
    results, outputs, staged = refs[:n], refs[n : 2 * n], refs[2 * n : 3 * n]
    came, went = refs[3 * n :]
    reads = [pltpu.make_async_copy(results[i], staged[i], came.at[i]) for i in range(n)]
    writes = [pltpu.make_async_copy(staged[i], outputs[i], went.at[i]) for i in range(n)]
    for read in reads:
        read.start()
    for read, write in zip(reads, writes):
        read.wait()
        write.start()
    for write in writes:
        write.wait()


def on_device(
    attn_values,
    attn_exponents,
    hidden_values,
    hidden_exponents,
    attn_out_grad,
    mlp_out_grad,
    attn_weight,
    mlp_weight,
):
    tokens, width = attn_out_grad.shape
    rows_a, rows_m = attn_weight.shape[0], mlp_weight.shape[0]
    rows = rows_a + rows_m
    factor = float(tokens * N) ** (-0.5)
    vmem = pl.BlockSpec(memory_space=pltpu.VMEM)
    hbm = pl.BlockSpec(memory_space=pl.ANY)
    dma = pltpu.SemaphoreType.DMA
    inputs = (
        attn_values.T,
        hidden_values.T,
        attn_exponents.T,
        hidden_exponents.T,
        attn_out_grad,
        mlp_out_grad,
        attn_weight,
        mlp_weight,
    )
    shapes = (
        jax.ShapeDtypeStruct((rows_a, tokens), BF16),
        jax.ShapeDtypeStruct((rows_m, tokens), BF16),
        jax.ShapeDtypeStruct((rows_a, width), BF16),
        jax.ShapeDtypeStruct((rows_m, width), BF16),
    )
    results = pl.pallas_call(
        functools.partial(kernel, factor),
        out_shape=shapes,
        in_specs=[hbm] * 8,
        out_specs=[vmem] * 4,
        scratch_shapes=[
            *[pltpu.VMEM(a.shape, a.dtype) for a in inputs[:6]],
            pltpu.VMEM((rows, width), BF16),
            pltpu.VMEM((rows, tokens), BF16),
            pltpu.VMEM((N, rows, tokens), BF16),
            pltpu.VMEM((N, rows, width), BF16),
            pltpu.VMEM((N, rows, width), BF16),
            pltpu.VMEM((N, rows, width), F32),
            pltpu.VMEM((NX, rows, tokens), F32),
            *[pltpu.VMEM((NX, rows, tokens), BF16)] * 4,
            pltpu.VMEM((rows, tokens), F32),
            dma((8,)),
            *[dma((N, CHUNKS))] * 4,
            *[dma((NX, PIECES))] * 8,
        ],
        compiler_params=pltpu.CompilerParams(
            collective_id=0, has_side_effects=True, vmem_limit_bytes=56 * 2**20
        ),
    )(*inputs)
    dxa, dxm, dwa, dwm = pl.pallas_call(
        write_out,
        out_shape=shapes,
        in_specs=[hbm] * 4,
        out_specs=[hbm] * 4,
        scratch_shapes=[*[pltpu.VMEM(a.shape, a.dtype) for a in shapes], dma((4,)), dma((4,))],
    )(*results)
    return (dxa.T, dxm.T, dwa, dwm)


def solution(mesh):
    placed = (
        P("gy", ("gx", "gz")),
        P("gy", "gx"),
        P("gy", ("gx", "gz")),
        P("gy", "gx"),
        P("gy", "gz"),
        P("gy", "gz"),
        P(("gx", "gy"), "gz"),
        P(("gx", "gy"), "gz"),
    )
    return jax.shard_map(
        on_device,
        mesh=mesh,
        in_specs=placed,
        out_specs=(
            P("gy", ("gx", "gz")),
            P("gy", ("gx", "gz")),
            P(("gx", "gy"), "gz"),
            P(("gx", "gy"), "gz"),
        ),
        check_vma=False,
    )
```

```python
import functools

import jax
import jax.numpy as jnp
from jax import lax
from jax.experimental import pallas as pl
from jax.experimental.pallas import tpu as pltpu
from jax.sharding import PartitionSpec as P

BLOCK = 128
N = 8
NX = 4
CHUNKS = 3
PIECES = 3
MESH = pl.DeviceIdType.MESH
F32 = jnp.float32
BF16 = jnp.bfloat16


def when(condition, *actions):
    @pl.when(condition)
    def _():
        for action in actions:
            action()


def kernel(
    factor, xa_in, xm_in, ea_in, em_in, ga_in, gm_in, wa_in, wm_in, dxa, dxm, dwa, dwm,
    xa, xm, ea, em, ga, gm, w, xt, xf, ru, rd, p, qk, qs, qc, qp, qr, total,
    ins, us, ur, ds, dr, xs, xr, cs, cr, qcs, qcr, qxs, qxr,
):
    gx, k, gz = lax.axis_index("gx"), lax.axis_index("gy"), lax.axis_index("gz")
    x, c = gz // 2, gz % 2
    sib = (gx, k, 2 * x + 1 - c)
    rows_a, rows_m = wa_in.shape[0], wm_in.shape[0]
    rows = rows_a + rows_m
    step = rows // CHUNKS
    piece = rows // PIECES
    above, below = (gx, jnp.minimum(k + 1, N - 1), gz), (gx, jnp.maximum(k - 1, 0), gz)

    def chip(other):
        return (gx, k, 2 * other + c)

    barrier = pltpu.get_barrier_semaphore()

    def greet(device):
        pl.semaphore_signal(barrier, inc=1, device_id=device, device_id_type=MESH)

    when(k < N - 1, lambda: greet(above))
    when(k > 0, lambda: greet(below))
    greet(sib)
    for d in (1, 2, 3):
        greet(chip((x + d) % NX))

    loads = [
        pltpu.make_async_copy(src, dst, ins.at[i])
        for i, (src, dst) in enumerate(
            (
                (xa_in, xa), (ea_in, ea), (xm_in, xm), (em_in, em), (ga_in, ga), (gm_in, gm),
                (wa_in, w.at[pl.ds(0, rows_a)]), (wm_in, w.at[pl.ds(rows_a, rows_m)]),
            )
        )
    ]
    for load in loads:
        load.start()
    pl.semaphore_wait(barrier, NX + (k < N - 1).astype(jnp.int32) + (k > 0).astype(jnp.int32))

    def remote(src, dst, send, recv, device):
        return pltpu.make_async_remote_copy(
            src_ref=src, dst_ref=dst, send_sem=send, recv_sem=recv, device_id=device, device_id_type=MESH
        )

    def up(s, i):
        at = pl.ds(i * step, step)
        index = (k - s + N) % N
        return remote(ru.at[index, at], ru.at[index, at], us.at[s, i], ur.at[s, i], above)

    def down(s, i):
        at = pl.ds(i * step, step)
        index = (k + s) % N
        return remote(rd.at[index, at], rd.at[index, at], ds.at[s, i], dr.at[s, i], below)

    def x_copy(d, h):
        at = pl.ds(h * piece, piece)
        return remote(xt.at[at], xf.at[gz, at], xs.at[d, h], xr.at[d, h], chip((x + d) % NX))

    def core_copy(d, h):
        at = pl.ds(h * piece, piece)
        index = 2 * ((x - d + NX) % NX) + c
        source = xt.at[at] if d == 0 else xf.at[index, at]
        return remote(source, xf.at[index, at], cs.at[d, h], cr.at[d, h], sib)

    def remote_pass(d, h):
        at = pl.ds(h * piece, piece)
        index = 2 * ((x - d + NX) % NX) + c
        return remote(xf.at[index, at], xf.at[index, at], cs.at[d, h], cr.at[d, h], sib)

    def first_packet(i, buf, send, recv, device):
        lo, hi = i * step, (i + 1) * step
        cut = min(max(lo, rows_a), hi)
        if lo < cut:
            src = wa_in.at[pl.ds(lo, cut - lo)]
            remote(src, buf.at[k, pl.ds(lo, cut - lo)], send.at[0, i], recv.at[0, i], device).start()
        if cut < hi:
            src = wm_in.at[pl.ds(cut - rows_a, hi - cut)]
            remote(src, buf.at[k, pl.ds(cut, hi - cut)], send.at[0, i], recv.at[0, i], device).start()

    for i in range(CHUNKS):
        when(k < N - 1, lambda: first_packet(i, ru, us, ur, above))
        when(k > 0, lambda: first_packet(i, rd, ds, dr, below))

    for load in loads[:4]:
        load.wait()

    def scaled(values, exponents, at, size, first):
        row = (gz * values.shape[0] + at) // BLOCK
        scale = jnp.exp2(exponents[pl.ds(row, 1), :].astype(F32))
        xt[first + at : first + at + size] = (values[at : at + size].astype(F32) * scale).astype(BF16)

    unit = 32
    for at in range(0, rows_a, unit):
        scaled(xa, ea, at, unit, 0)
    for at in range(0, rows_m, unit):
        scaled(xm, em, at, unit, rows_a)

    ahead = jnp.where(k < N // 2, NX - 1, 0)
    held = ((k == 0) | (k == N - 1)) & (x != ahead)

    def x_start():
        for h in range(PIECES):
            for d in (1, 3, 2):
                x_copy(d, h).start()

    when(jnp.logical_not(held), x_start)
    for h in range(PIECES):
        core_copy(0, h).start()
    xf[gz] = xt[...]
    for load in loads[4:]:
        load.wait()

    def to_core(xj, h):
        at = pl.ds(h * piece, piece)
        return remote(qs.at[xj, at], qc.at[xj, at], qcs.at[xj, h], qcr.at[xj, h], sib)

    def to_chip(xj, h, sender):
        at = pl.ds(h * piece, piece)
        return remote(qp.at[xj, at], qr.at[sender, at], qxs.at[xj, h], qxr.at[sender, h], chip(xj))

    def grad_dot(source, j, pieces=range(PIECES)):
        dims = (((1,), (1,)), ((), ()))
        xj, cj = j // 2, j % 2
        lo, hi = pieces[0] * piece, (pieces[-1] + 1) * piece
        cut = min(max(lo, rows_a), hi)
        for first, end, grads in ((lo, cut, ga), (cut, hi, gm)):
            if first < end:
                part = lax.dot_general(source[first:end], grads[...], dims, preferred_element_type=F32)

                @pl.when(cj == c)
                def _():
                    qk[xj, first:end] = part

                @pl.when(cj != c)
                def _():
                    qs[xj, first:end] = part.astype(BF16)

        @pl.when(cj != c)
        def _():
            for h in pieces:
                to_core(xj, h).start()

    def pair_sum(j, pieces=range(PIECES)):
        xj, cj = j // 2, j % 2

        @pl.when(cj == c)
        def _():
            for h in pieces:
                lo, hi = h * piece, (h + 1) * piece
                to_core(xj, h).wait_recv()

                @pl.when(xj != x)
                def _():
                    qp[xj, lo:hi] = (qk[xj, lo:hi] + qc[xj, lo:hi].astype(F32)).astype(BF16)
                    to_chip(xj, h, x).start()

                @pl.when(xj == x)
                def _():
                    total[lo:hi] = qk[xj, lo:hi] + qc[xj, lo:hi].astype(F32)

    def weight_dot(index, lo, hi):
        if lo < rows_a:
            p[index, lo:rows_a] = jnp.dot(xf[index, lo:rows_a], ga[...], preferred_element_type=F32)
            lo = rows_a
        p[index, lo:hi] = jnp.dot(xf[index, lo:hi], gm[...], preferred_element_type=F32)

    def sides(s):
        return (
            (ru, up, k == 0, k == N - 1, (k - s + N) % N, s <= k),
            (rd, down, k == N - 1, k == 0, (k + s) % N, s <= N - 1 - k),
        )

    def forward(s, i, kinds="ws"):
        at = pl.ds(i * step, step)
        for buf, copy, first, last, index, weights in sides(s):
            if "w" in kinds:
                @pl.when(weights)
                def _():
                    copy(s - 1, i).wait_recv()
                    when(jnp.logical_not(last), lambda: copy(s, i).start())

            if "s" in kinds:
                @pl.when(jnp.logical_not(weights | last))
                def _():
                    @pl.when(jnp.logical_not(first))
                    def _():
                        copy(s - 1, i).wait_recv()
                        buf[index, at] = (p[index, at] + buf[index, at].astype(F32)).astype(BF16)

                    @pl.when(first)
                    def _():
                        buf[index, at] = p[index, at].astype(BF16)

                    copy(s, i).start()

    def input_part(s, side, pieces=range(PIECES)):
        j = k - s if side == 0 else k + s
        when((j >= 0) & (j < N), lambda: grad_dot((ru, rd)[side].at[j], j, pieces))

    def input_sums(s, pieces=range(PIECES)):
        for j in (k - s, k + s):
            when((j >= 0) & (j < N), lambda: pair_sum(j, pieces))

    def next_partial(s, side, lo=0, hi=rows):
        _, _, _, last, index, weights = sides(s)[side]
        when(jnp.logical_not(weights | last), lambda: weight_dot(index, lo, hi))

    def x_wait(n, h):
        d = (x - jnp.where(k < N // 2, NX - 1 - n, n) + NX) % NX

        @pl.when(d != 0)
        def _():
            x_copy(d, h).wait_recv()
            remote_pass(d, h).start()

    def core_wait(n, h):
        d = (x - jnp.where(k < N // 2, NX - 1 - n, n) + NX) % NX
        remote_pass(d, h).wait_recv()

    def first_sums(h):
        for side in range(2):
            next_partial(1, side, h * piece, (h + 1) * piece)
        for i in range(h * CHUNKS // PIECES, (h + 1) * CHUNKS // PIECES):
            forward(1, i, "s")

    grad_dot(w, k)
    forward(1, 0, "w")
    forward(1, 1, "w")
    x_wait(0, 0)
    when(held, x_start)
    core_wait(0, 0)
    first_sums(0)
    forward(1, 2, "w")
    x_wait(0, 1)
    core_wait(0, 1)
    first_sums(1)
    x_wait(0, 2)
    core_wait(0, 2)
    first_sums(2)
    for side in range(2):
        next_partial(2, side)

    forward(2, 0)
    for h in range(PIECES):
        x_wait(1, h)
    input_part(1, 0)
    forward(2, 1)
    for h in range(PIECES):
        core_wait(1, h)
    for h in range(PIECES):
        x_wait(2, h)
    input_part(1, 1)
    for h in range(PIECES):
        x_wait(3, h)
    next_partial(3, 0)
    forward(2, 2)
    next_partial(3, 1)
    for n in (2, 3):
        for h in range(PIECES):
            core_wait(n, h)
    pair_sum(k)

    def gone(s, i):
        when(k < N - 1, lambda: up(s, i).wait_send())
        when(k > 0, lambda: down(s, i).wait_send())

    def body(s, carry):
        forward(s, 0)
        input_part(s - 1, 0)
        input_part(s - 1, 1)
        gone(s - 3, 0)
        forward(s, 1)
        next_partial(s + 1, 0)
        next_partial(s + 1, 1)
        gone(s - 3, 1)
        forward(s, 2)
        input_sums(s - 2)
        gone(s - 3, 2)
        return carry

    lax.fori_loop(3, N - 2, body, 0)

    input_sums(N - 4)
    for s in (N - 2, N - 1):
        for h in range(PIECES):
            for i in range(h * CHUNKS // PIECES, (h + 1) * CHUNKS // PIECES):
                forward(s, i)
                gone(s - 3, i)
            for side in range(2):
                input_part(s, side, (h,))
                if s == N - 2:
                    next_partial(s + 1, side, h * piece, (h + 1) * piece)
            if s == N - 2 and h < 2:
                input_part(s - 1, h)
            if h > 0:
                input_sums(s, (h - 1,))
        if s == N - 2:
            input_sums(s - 1)
        input_sums(s, (PIECES - 1,))
    weight_dot(k, 0, rows)
    for d in (1, 2, 3):
        for h in range(PIECES):
            x_copy(d, h).wait_send()
    for d in range(NX):
        for h in range(PIECES):
            core_copy(d, h).wait_send()
    for s in (N - 3, N - 2):
        for i in range(CHUNKS):
            gone(s, i)

    def last_sums():
        for d in (1, 3, 2):
            other = (x - d + NX) % NX
            for h in range(PIECES):
                to_chip(other, h, other).wait_recv()
            total[...] = total[...] + qr[other].astype(F32)
        dxa[...] = total[:rows_a].astype(BF16)
        dxm[...] = total[rows_a:].astype(BF16)

    def last_rows(start, stop):
        for i in range(start, stop):
            lo, hi = i * step, (i + 1) * step
            for buf, copy, none in ((ru, up, k == 0), (rd, down, k == N - 1)):
                @pl.when(jnp.logical_not(none))
                def _():
                    copy(N - 1, i).wait_recv()
                    p[k, lo:hi] = p[k, lo:hi] + buf[k, lo:hi].astype(F32)

            cut = min(max(lo, rows_a), hi)
            if lo < cut:
                dwa[lo:cut] = (p[k, lo:cut] * factor).astype(BF16)
            if cut < hi:
                dwm[cut - rows_a : hi - rows_a] = (p[k, cut:hi] * factor).astype(BF16)

    for d in range(NX):
        for h in range(PIECES):
            to_core(d, h).wait_send()
    last_rows(0, 2)
    last_sums()
    for d in (1, 2, 3):
        for h in range(PIECES):
            to_chip((x + d) % NX, h, x).wait_send()
    gone(N - 1, 0)
    gone(N - 1, 1)
    last_rows(2, CHUNKS)
    gone(N - 1, CHUNKS - 1)


def write_out(*refs):
    n = (len(refs) - 2) // 3
    results, outputs, staged = refs[:n], refs[n : 2 * n], refs[2 * n : 3 * n]
    came, went = refs[3 * n :]
    reads = [pltpu.make_async_copy(results[i], staged[i], came.at[i]) for i in range(n)]
    writes = [pltpu.make_async_copy(staged[i], outputs[i], went.at[i]) for i in range(n)]
    for read in reads:
        read.start()
    for read, write in zip(reads, writes):
        read.wait()
        write.start()
    for write in writes:
        write.wait()


def on_device(
    attn_values,
    attn_exponents,
    hidden_values,
    hidden_exponents,
    attn_out_grad,
    mlp_out_grad,
    attn_weight,
    mlp_weight,
):
    tokens, width = attn_out_grad.shape
    rows_a, rows_m = attn_weight.shape[0], mlp_weight.shape[0]
    rows = rows_a + rows_m
    factor = float(tokens * N) ** (-0.5)
    vmem = pl.BlockSpec(memory_space=pltpu.VMEM)
    hbm = pl.BlockSpec(memory_space=pl.ANY)
    dma = pltpu.SemaphoreType.DMA
    inputs = (
        attn_values.T,
        hidden_values.T,
        attn_exponents.T,
        hidden_exponents.T,
        attn_out_grad,
        mlp_out_grad,
        attn_weight,
        mlp_weight,
    )
    shapes = (
        jax.ShapeDtypeStruct((rows_a, tokens), BF16),
        jax.ShapeDtypeStruct((rows_m, tokens), BF16),
        jax.ShapeDtypeStruct((rows_a, width), BF16),
        jax.ShapeDtypeStruct((rows_m, width), BF16),
    )
    results = pl.pallas_call(
        functools.partial(kernel, factor),
        out_shape=shapes,
        in_specs=[hbm] * 8,
        out_specs=[vmem] * 4,
        scratch_shapes=[
            *[pltpu.VMEM(a.shape, a.dtype) for a in inputs[:6]],
            pltpu.VMEM((rows, width), BF16),
            pltpu.VMEM((rows, tokens), BF16),
            pltpu.VMEM((N, rows, tokens), BF16),
            pltpu.VMEM((N, rows, width), BF16),
            pltpu.VMEM((N, rows, width), BF16),
            pltpu.VMEM((N, rows, width), F32),
            pltpu.VMEM((NX, rows, tokens), F32),
            *[pltpu.VMEM((NX, rows, tokens), BF16)] * 4,
            pltpu.VMEM((rows, tokens), F32),
            dma((8,)),
            *[dma((N, CHUNKS))] * 4,
            *[dma((NX, PIECES))] * 8,
        ],
        compiler_params=pltpu.CompilerParams(
            collective_id=0, has_side_effects=True, vmem_limit_bytes=56 * 2**20
        ),
    )(*inputs)
    dxa, dxm, dwa, dwm = pl.pallas_call(
        write_out,
        out_shape=shapes,
        in_specs=[hbm] * 4,
        out_specs=[hbm] * 4,
        scratch_shapes=[*[pltpu.VMEM(a.shape, a.dtype) for a in shapes], dma((4,)), dma((4,))],
    )(*results)
    return (dxa.T, dxm.T, dwa, dwm)


def solution(mesh):
    placed = (
        P("gy", ("gx", "gz")),
        P("gy", "gx"),
        P("gy", ("gx", "gz")),
        P("gy", "gx"),
        P("gy", "gz"),
        P("gy", "gz"),
        P(("gx", "gy"), "gz"),
        P(("gx", "gy"), "gz"),
    )
    return jax.shard_map(
        on_device,
        mesh=mesh,
        in_specs=placed,
        out_specs=(
            P("gy", ("gx", "gz")),
            P("gy", ("gx", "gz")),
            P(("gx", "gy"), "gz"),
            P(("gx", "gy"), "gz"),
        ),
        check_vma=False,
    )
```

```python
import functools

import jax
import jax.numpy as jnp
from jax import lax
from jax.experimental import pallas as pl
from jax.experimental.pallas import tpu as pltpu
from jax.sharding import PartitionSpec as P

BLOCK = 128
N = 8
NX = 4
CHUNKS = 3
PIECES = 3
MESH = pl.DeviceIdType.MESH
F32 = jnp.float32
BF16 = jnp.bfloat16


def when(condition, *actions):
    @pl.when(condition)
    def _():
        for action in actions:
            action()


def kernel(
    factor, xa_in, xm_in, ea_in, em_in, ga_in, gm_in, wa_in, wm_in, dxa_out, dxm_out, dwa_out, dwm_out,
    dxa, dxm, dwa, dwm,
    xa, xm, ea, em, ga, gm, w, xt, xf, ru, rd, p, qk, qs, qc, qp, qr, total,
    ins, outs, us, ur, ds, dr, xs, xr, cs, cr, qcs, qcr, qxs, qxr,
):
    gx, k, gz = lax.axis_index("gx"), lax.axis_index("gy"), lax.axis_index("gz")
    x, c = gz // 2, gz % 2
    sib = (gx, k, 2 * x + 1 - c)
    rows_a, rows_m = wa_in.shape[0], wm_in.shape[0]
    rows = rows_a + rows_m
    step = rows // CHUNKS
    piece = rows // PIECES
    above, below = (gx, jnp.minimum(k + 1, N - 1), gz), (gx, jnp.maximum(k - 1, 0), gz)

    def chip(other):
        return (gx, k, 2 * other + c)

    barrier = pltpu.get_barrier_semaphore()

    def greet(device):
        pl.semaphore_signal(barrier, inc=1, device_id=device, device_id_type=MESH)

    greet(sib)
    for d in (1, 2, 3):
        greet(chip((x + d) % NX))
    when(k < N - 1, lambda: greet(above))
    when(k > 0, lambda: greet(below))

    loads = [
        pltpu.make_async_copy(src, dst, ins.at[i])
        for i, (src, dst) in enumerate(
            (
                (xa_in, xa), (ea_in, ea), (xm_in, xm), (em_in, em), (ga_in, ga), (gm_in, gm),
                (wa_in, w.at[pl.ds(0, rows_a)]), (wm_in, w.at[pl.ds(rows_a, rows_m)]),
            )
        )
    ]
    for load in loads:
        load.start()
    pl.semaphore_wait(barrier, NX + (k < N - 1).astype(jnp.int32) + (k > 0).astype(jnp.int32))

    def remote(src, dst, send, recv, device):
        return pltpu.make_async_remote_copy(
            src_ref=src, dst_ref=dst, send_sem=send, recv_sem=recv, device_id=device, device_id_type=MESH
        )

    def up(s, i):
        at = pl.ds(i * step, step)
        index = (k - s + N) % N
        return remote(ru.at[index, at], ru.at[index, at], us.at[s, i], ur.at[s, i], above)

    def down(s, i):
        at = pl.ds(i * step, step)
        index = (k + s) % N
        return remote(rd.at[index, at], rd.at[index, at], ds.at[s, i], dr.at[s, i], below)

    def x_copy(d, h):
        at = pl.ds(h * piece, piece)
        return remote(xt.at[at], xf.at[gz, at], xs.at[d, h], xr.at[d, h], chip((x + d) % NX))

    def core_copy(d, h):
        at = pl.ds(h * piece, piece)
        index = 2 * ((x - d + NX) % NX) + c
        source = xt.at[at] if d == 0 else xf.at[index, at]
        return remote(source, xf.at[index, at], cs.at[d, h], cr.at[d, h], sib)

    def remote_pass(d, h):
        at = pl.ds(h * piece, piece)
        index = 2 * ((x - d + NX) % NX) + c
        return remote(xf.at[index, at], xf.at[index, at], cs.at[d, h], cr.at[d, h], sib)

    def first_packet(i, buf, send, recv, device):
        lo, hi = i * step, (i + 1) * step
        cut = min(max(lo, rows_a), hi)
        if lo < cut:
            src = wa_in.at[pl.ds(lo, cut - lo)]
            remote(src, buf.at[k, pl.ds(lo, cut - lo)], send.at[0, i], recv.at[0, i], device).start()
        if cut < hi:
            src = wm_in.at[pl.ds(cut - rows_a, hi - cut)]
            remote(src, buf.at[k, pl.ds(cut, hi - cut)], send.at[0, i], recv.at[0, i], device).start()

    for i in range(CHUNKS):
        when(k < N - 1, lambda: first_packet(i, ru, us, ur, above))
        when(k > 0, lambda: first_packet(i, rd, ds, dr, below))

    for load in loads[:4]:
        load.wait()

    def scaled(values, exponents, at, size, first):
        row = (gz * values.shape[0] + at) // BLOCK
        scale = jnp.exp2(exponents[pl.ds(row, 1), :].astype(F32))
        xt[first + at : first + at + size] = (values[at : at + size].astype(F32) * scale).astype(BF16)

    unit = 32
    for at in range(0, rows_a, unit):
        scaled(xa, ea, at, unit, 0)
    for at in range(0, rows_m, unit):
        scaled(xm, em, at, unit, rows_a)

    ahead = jnp.where(k < N // 2, NX - 1, 0)
    held = ((k == 0) | (k == N - 1)) & (x != ahead)

    def x_start():
        for h in range(PIECES):
            for d in (1, 3, 2):
                x_copy(d, h).start()

    when(jnp.logical_not(held), x_start)
    for h in range(PIECES):
        core_copy(0, h).start()
    xf[gz] = xt[...]
    for load in loads[4:]:
        load.wait()

    def to_core(xj, h):
        at = pl.ds(h * piece, piece)
        return remote(qs.at[xj, at], qc.at[xj, at], qcs.at[xj, h], qcr.at[xj, h], sib)

    def to_chip(xj, h, sender):
        at = pl.ds(h * piece, piece)
        return remote(qp.at[xj, at], qr.at[sender, at], qxs.at[xj, h], qxr.at[sender, h], chip(xj))

    def grad_dot(source, j, pieces=range(PIECES)):
        dims = (((1,), (1,)), ((), ()))
        xj, cj = j // 2, j % 2
        lo, hi = pieces[0] * piece, (pieces[-1] + 1) * piece
        cut = min(max(lo, rows_a), hi)
        for first, end, grads in ((lo, cut, ga), (cut, hi, gm)):
            if first < end:
                part = lax.dot_general(source[first:end], grads[...], dims, preferred_element_type=F32)

                @pl.when(cj == c)
                def _():
                    qk[xj, first:end] = part

                @pl.when(cj != c)
                def _():
                    qs[xj, first:end] = part.astype(BF16)

        @pl.when(cj != c)
        def _():
            for h in pieces:
                to_core(xj, h).start()

    def pair_sum(j, pieces=range(PIECES)):
        xj, cj = j // 2, j % 2

        @pl.when(cj == c)
        def _():
            for h in pieces:
                lo, hi = h * piece, (h + 1) * piece
                to_core(xj, h).wait_recv()

                @pl.when(xj != x)
                def _():
                    qp[xj, lo:hi] = (qk[xj, lo:hi] + qc[xj, lo:hi].astype(F32)).astype(BF16)
                    to_chip(xj, h, x).start()

                @pl.when(xj == x)
                def _():
                    total[lo:hi] = qk[xj, lo:hi] + qc[xj, lo:hi].astype(F32)

    def weight_dot(index, lo, hi):
        if lo < rows_a:
            p[index, lo:rows_a] = jnp.dot(xf[index, lo:rows_a], ga[...], preferred_element_type=F32)
            lo = rows_a
        p[index, lo:hi] = jnp.dot(xf[index, lo:hi], gm[...], preferred_element_type=F32)

    def sides(s):
        return (
            (ru, up, k == 0, k == N - 1, (k - s + N) % N, s <= k),
            (rd, down, k == N - 1, k == 0, (k + s) % N, s <= N - 1 - k),
        )

    def forward(s, i, kinds="ws"):
        at = pl.ds(i * step, step)
        for buf, copy, first, last, index, weights in sides(s):
            if "w" in kinds:
                @pl.when(weights)
                def _():
                    copy(s - 1, i).wait_recv()
                    when(jnp.logical_not(last), lambda: copy(s, i).start())

            if "s" in kinds:
                @pl.when(jnp.logical_not(weights | last))
                def _():
                    @pl.when(jnp.logical_not(first))
                    def _():
                        copy(s - 1, i).wait_recv()
                        buf[index, at] = (p[index, at] + buf[index, at].astype(F32)).astype(BF16)

                    @pl.when(first)
                    def _():
                        buf[index, at] = p[index, at].astype(BF16)

                    copy(s, i).start()

    def input_part(s, side, pieces=range(PIECES)):
        j = k - s if side == 0 else k + s
        when((j >= 0) & (j < N), lambda: grad_dot((ru, rd)[side].at[j], j, pieces))

    def input_sums(s, pieces=range(PIECES)):
        for j in (k - s, k + s):
            when((j >= 0) & (j < N), lambda: pair_sum(j, pieces))

    def next_partial(s, side, lo=0, hi=rows):
        _, _, _, last, index, weights = sides(s)[side]
        when(jnp.logical_not(weights | last), lambda: weight_dot(index, lo, hi))

    def x_wait(n, h):
        d = (x - jnp.where(k < N // 2, NX - 1 - n, n) + NX) % NX

        @pl.when(d != 0)
        def _():
            x_copy(d, h).wait_recv()
            remote_pass(d, h).start()

    def core_wait(n, h):
        d = (x - jnp.where(k < N // 2, NX - 1 - n, n) + NX) % NX
        remote_pass(d, h).wait_recv()

    def first_sums(h):
        for side in range(2):
            next_partial(1, side, h * piece, (h + 1) * piece)
        for i in range(h * CHUNKS // PIECES, (h + 1) * CHUNKS // PIECES):
            forward(1, i, "s")

    grad_dot(w, k)
    forward(1, 0, "w")
    x_wait(0, 0)
    when(held, x_start)
    core_wait(0, 0)
    first_sums(0)
    forward(1, 1, "w")
    x_wait(0, 1)
    core_wait(0, 1)
    first_sums(1)
    forward(1, 2, "w")
    x_wait(0, 2)
    core_wait(0, 2)
    first_sums(2)
    for side in range(2):
        next_partial(2, side)

    forward(2, 0)
    for h in range(PIECES):
        x_wait(1, h)
    for h in range(PIECES):
        core_wait(1, h)
    input_part(1, 0)
    forward(2, 1)
    for h in range(PIECES):
        x_wait(2, h)
    input_part(1, 1)
    for h in range(PIECES):
        x_wait(3, h)
    next_partial(3, 0)
    forward(2, 2)
    next_partial(3, 1)
    for n in (2, 3):
        for h in range(PIECES):
            core_wait(n, h)
    pair_sum(k)

    def gone(s, i):
        when(k < N - 1, lambda: up(s, i).wait_send())
        when(k > 0, lambda: down(s, i).wait_send())

    def body(s, carry):
        forward(s, 0)
        input_part(s - 1, 0)
        input_part(s - 1, 1)
        gone(s - 3, 0)
        forward(s, 1)
        next_partial(s + 1, 0)
        next_partial(s + 1, 1)
        gone(s - 3, 1)
        forward(s, 2)
        input_sums(s - 2)
        gone(s - 3, 2)
        return carry

    lax.fori_loop(3, N - 2, body, 0)

    input_sums(N - 4)
    for s in (N - 2, N - 1):
        for h in range(PIECES):
            for i in range(h * CHUNKS // PIECES, (h + 1) * CHUNKS // PIECES):
                forward(s, i)
                gone(s - 3, i)
            for side in range(2):
                input_part(s, side, (h,))
                if s == N - 2:
                    next_partial(s + 1, side, h * piece, (h + 1) * piece)
            if s == N - 2 and h < 2:
                input_part(s - 1, h)
            if h > 0:
                input_sums(s, (h - 1,))
        if s == N - 2:
            input_sums(s - 1)
        input_sums(s, (PIECES - 1,))
    weight_dot(k, 0, rows)
    for d in (1, 2, 3):
        for h in range(PIECES):
            x_copy(d, h).wait_send()
    for d in range(NX):
        for h in range(PIECES):
            core_copy(d, h).wait_send()
    for s in (N - 3, N - 2):
        for i in range(CHUNKS):
            gone(s, i)

    def results(src, dst, i):
        return pltpu.make_async_copy(src, dst, outs.at[i])

    def last_sums():
        for d in (1, 3, 2):
            other = (x - d + NX) % NX
            for h in range(PIECES):
                to_chip(other, h, other).wait_recv()
            total[...] = total[...] + qr[other].astype(F32)
        dxa[...] = total[:rows_a].astype(BF16)
        dxm[...] = total[rows_a:].astype(BF16)
        results(dxa, dxa_out, 0).start()
        results(dxm, dxm_out, 1).start()

    def last_rows(start, stop):
        for i in range(start, stop):
            lo, hi = i * step, (i + 1) * step
            for buf, copy, none in ((ru, up, k == 0), (rd, down, k == N - 1)):
                @pl.when(jnp.logical_not(none))
                def _():
                    copy(N - 1, i).wait_recv()
                    p[k, lo:hi] = p[k, lo:hi] + buf[k, lo:hi].astype(F32)

            cut = min(max(lo, rows_a), hi)
            if lo < cut:
                dwa[lo:cut] = (p[k, lo:cut] * factor).astype(BF16)
            if cut < hi:
                dwm[cut - rows_a : hi - rows_a] = (p[k, cut:hi] * factor).astype(BF16)
            for copy in row_copies(i):
                copy.start()

    def row_copies(i):
        lo, hi = i * step, (i + 1) * step
        cut = min(max(lo, rows_a), hi)
        copies = []
        if lo < cut:
            at = pl.ds(lo, cut - lo)
            copies.append(results(dwa.at[at], dwa_out.at[at], 2))
        if cut < hi:
            at = pl.ds(cut - rows_a, hi - cut)
            copies.append(results(dwm.at[at], dwm_out.at[at], 3 + i))
        return copies

    for d in range(NX):
        for h in range(PIECES):
            to_core(d, h).wait_send()
    last_rows(0, 2)
    last_sums()
    for d in (1, 2, 3):
        for h in range(PIECES):
            to_chip((x + d) % NX, h, x).wait_send()
    gone(N - 1, 0)
    gone(N - 1, 1)
    last_rows(2, CHUNKS)
    gone(N - 1, CHUNKS - 1)
    results(dxa, dxa_out, 0).wait()
    results(dxm, dxm_out, 1).wait()
    for i in range(CHUNKS):
        for copy in row_copies(i):
            copy.wait()


def write_out(*refs):
    n = (len(refs) - 2) // 3
    results, outputs, staged = refs[:n], refs[n : 2 * n], refs[2 * n : 3 * n]
    came, went = refs[3 * n :]
    reads = [pltpu.make_async_copy(results[i], staged[i], came.at[i]) for i in range(n)]
    writes = [pltpu.make_async_copy(staged[i], outputs[i], went.at[i]) for i in range(n)]
    for read in reads:
        read.start()
    for read, write in zip(reads, writes):
        read.wait()
        write.start()
    for write in writes:
        write.wait()


def on_device(
    attn_values,
    attn_exponents,
    hidden_values,
    hidden_exponents,
    attn_out_grad,
    mlp_out_grad,
    attn_weight,
    mlp_weight,
):
    tokens, width = attn_out_grad.shape
    rows_a, rows_m = attn_weight.shape[0], mlp_weight.shape[0]
    rows = rows_a + rows_m
    factor = float(tokens * N) ** (-0.5)
    vmem = pl.BlockSpec(memory_space=pltpu.VMEM)
    hbm = pl.BlockSpec(memory_space=pl.ANY)
    dma = pltpu.SemaphoreType.DMA
    inputs = (
        attn_values.T,
        hidden_values.T,
        attn_exponents.T,
        hidden_exponents.T,
        attn_out_grad,
        mlp_out_grad,
        attn_weight,
        mlp_weight,
    )
    shapes = (
        jax.ShapeDtypeStruct((rows_a, tokens), BF16),
        jax.ShapeDtypeStruct((rows_m, tokens), BF16),
        jax.ShapeDtypeStruct((rows_a, width), BF16),
        jax.ShapeDtypeStruct((rows_m, width), BF16),
    )
    results = pl.pallas_call(
        functools.partial(kernel, factor),
        out_shape=shapes,
        in_specs=[hbm] * 8,
        out_specs=[hbm] * 4,
        scratch_shapes=[
            *[pltpu.VMEM(a.shape, a.dtype) for a in shapes],
            *[pltpu.VMEM(a.shape, a.dtype) for a in inputs[:6]],
            pltpu.VMEM((rows, width), BF16),
            pltpu.VMEM((rows, tokens), BF16),
            pltpu.VMEM((N, rows, tokens), BF16),
            pltpu.VMEM((N, rows, width), BF16),
            pltpu.VMEM((N, rows, width), BF16),
            pltpu.VMEM((N, rows, width), F32),
            pltpu.VMEM((NX, rows, tokens), F32),
            *[pltpu.VMEM((NX, rows, tokens), BF16)] * 4,
            pltpu.VMEM((rows, tokens), F32),
            dma((8,)),
            dma((3 + CHUNKS,)),
            *[dma((N, CHUNKS))] * 4,
            *[dma((NX, PIECES))] * 8,
        ],
        compiler_params=pltpu.CompilerParams(
            collective_id=0, has_side_effects=True, vmem_limit_bytes=56 * 2**20
        ),
    )(*inputs)
    dxa, dxm, dwa, dwm = pl.pallas_call(
        write_out,
        out_shape=shapes,
        in_specs=[hbm] * 4,
        out_specs=[hbm] * 4,
        scratch_shapes=[*[pltpu.VMEM(a.shape, a.dtype) for a in shapes], dma((4,)), dma((4,))],
    )(*results)
    return (dxa.T, dxm.T, dwa, dwm)


def solution(mesh):
    placed = (
        P("gy", ("gx", "gz")),
        P("gy", "gx"),
        P("gy", ("gx", "gz")),
        P("gy", "gx"),
        P("gy", "gz"),
        P("gy", "gz"),
        P(("gx", "gy"), "gz"),
        P(("gx", "gy"), "gz"),
    )
    return jax.shard_map(
        on_device,
        mesh=mesh,
        in_specs=placed,
        out_specs=(
            P("gy", ("gx", "gz")),
            P("gy", ("gx", "gz")),
            P(("gx", "gy"), "gz"),
            P(("gx", "gy"), "gz"),
        ),
        check_vma=False,
    )
```
